256 devices in a mesh: heads: 8 (over x, core), seq: 32 (over y, z).
Axes of the slice: x: 4, y: 4, z: 8, core: 2. Of those that a mesh axis runs over, the one named last changes fastest.
Arguments:
- layer_input: bfloat16 [16384, 3072], P('seq'), may hold values from -6 to 6
- query_preact: bfloat16 [16384, 4096], P('seq', 'heads'), may hold values from -6 to 6
- key_preact: bfloat16 [16384, 4096], P('seq', 'heads'), may hold values from -6 to 6
- value_rows: bfloat16 [16384, 4096], P('seq', 'heads'), may hold values from -6 to 6
- output_grad: bfloat16 [16384, 4096], P('seq', 'heads'), may hold values from -6 to 6
- log_decay: float32 [16384, 32], P('seq', 'heads'), may hold values from -2 to 0, as said below
Outputs:
- qweight_grad: float32 [3072, 4096], P('seq', 'heads')
- kweight_grad: float32 [3072, 4096], P('seq', 'heads')
- value_grad: bfloat16 [16384, 4096], P('seq', 'heads')
The draws below stay inside these ranges and needn't reach their ends.
Inputs may be any that keep to these rules, and one draw needn't show every extreme that they name: `log_decay`: negative at every position.
All inputs are finite; a program needn't handle non-finite values.
Results may differ from the reference program's by a relative error of at most 0.024.
Values may be sent and summed in bfloat16 or wider, within the bound.
No kernel may reach another device: no remote copies, remote signals or barrier semaphores. Data moves between devices by JAX's collectives and lax.ppermute only.
A program may use at most 128 MiB of HBM per device.

```python
import jax
import jax.numpy as jnp
from jax import lax

D = 3072
HEAD_DIM = 128
TOK_DEV = 512
BLOCK = 512
HEAD_COUNT = 32
TOKEN_COUNT = 16384
N_SEQ = 32


def draw_log_decay(key, part):
    key = jax.random.fold_in(key, 11)
    key_vectors = jax.random.split(key, 7)
    order = jax.random.permutation(key_vectors[0], HEAD_COUNT)
    slow = order < HEAD_COUNT // 2
    slow_rate = jnp.exp(jax.random.uniform(key_vectors[1], (HEAD_COUNT,), jnp.float32, jnp.log(0.02), jnp.log(0.3))) / TOKEN_COUNT
    fast_rate = jnp.exp(jax.random.uniform(key_vectors[2], (HEAD_COUNT,), jnp.float32, jnp.log(0.02), jnp.log(0.1)))
    decay_speeds = jnp.where(slow, slow_rate, fast_rate)
    devices = TOKEN_COUNT // TOK_DEV
    shard_multiplier = jnp.exp(jax.random.uniform(key_vectors[3], (devices, HEAD_COUNT), jnp.float32, jnp.log(0.5), jnp.log(2.0)))
    shard_multiplier = jnp.repeat(shard_multiplier, TOK_DEV, axis=0)
    position_multiplier = jnp.exp(jax.random.uniform(key_vectors[4], (TOKEN_COUNT, HEAD_COUNT), jnp.float32, jnp.log(0.5), jnp.log(2.0)))
    spike_locations = jax.random.randint(key_vectors[5], (3,), 0, TOKEN_COUNT)
    spike_retain = jax.random.uniform(key_vectors[6], (3, HEAD_COUNT), jnp.float32, 0.6, 0.8)
    spike_matches = (jnp.arange(TOKEN_COUNT)[:, None] == spike_locations[None, :]).astype(jnp.float32)
    spike_events = jnp.sum(spike_matches[:, :, None] * jnp.log(spike_retain)[None, :, :], axis=1)
    return -decay_speeds[None, :] * shard_multiplier * position_multiplier + spike_events


def spiked(drawn, stream_key, source, target, blocks, factor):
    owner, partner = [(jnp.arange(drawn.shape[dim]) // (drawn.shape[dim] // blocks)).reshape([-1 if axis == dim else 1 for axis in range(drawn.ndim)]) for dim in (source, target)]
    chosen = jax.random.permutation(stream_key, blocks)[partner]
    strong = (owner == chosen) | (owner == (partner + blocks // 2) % blocks)
    return jnp.where(strong, factor * drawn, drawn)


def block_levels(rng, dims, cuts, low, largest):
    factor_of = 1.0
    for axis_at, parts in cuts:
        steps = jax.random.uniform(jax.random.fold_in(jax.random.fold_in(rng, 6), axis_at), (parts,), jnp.float32, low / len(cuts), largest / len(cuts))
        factor_of = factor_of * jnp.repeat(jnp.exp(steps), dims[axis_at] // parts).reshape((-1,) + (1,) * (len(dims) - 1 - axis_at))
    return factor_of


def bell_draw(own_key, shape, deviation, limit, cuts=(), dtype=jnp.bfloat16):
    gain = block_levels(own_key, shape, cuts, -0.22, 0.18) if cuts else 1.0
    result = jax.random.normal(own_key, shape, jnp.float32) * deviation * gain
    return jnp.minimum(jnp.maximum(result, -limit), limit).astype(dtype)


def noise_with(rng, extent, width, most, cuts, heavy, held_as=jnp.bfloat16):
    entries = width * jax.random.normal(rng, extent, jnp.float32)
    if cuts:
        entries = entries * block_levels(rng, extent, cuts, -0.22, 0.18)
    return jnp.clip(spiked(entries, jax.random.fold_in(rng, 3), *heavy), -most, most).astype(held_as)


def setup_inputs(seed: int = 0) -> dict:
    streams_of = jax.random.split(jax.random.key(seed), 7)
    layer_input = noise_with(streams_of[0], (TOKEN_COUNT, D), 1.0, 6.0, ((0, 32),), (0, 1, 32, 2.75))
    query_preact = bell_draw(streams_of[1], (TOKEN_COUNT, HEAD_COUNT * HEAD_DIM), 1.0, 6.0, ((0, 32), (1, 8)))
    key_preact = bell_draw(streams_of[2], (TOKEN_COUNT, HEAD_COUNT * HEAD_DIM), 1.0, 6.0, ((0, 32), (1, 8)))
    value_rows = bell_draw(streams_of[3], (TOKEN_COUNT, HEAD_COUNT * HEAD_DIM), 1.0, 6.0, ((0, 32), (1, 8)))
    output_grad = bell_draw(streams_of[4], (TOKEN_COUNT, HEAD_COUNT * HEAD_DIM), 1.0, 6.0, ((0, 32), (1, 8)))
    log_decay = draw_log_decay(jax.random.fold_in(streams_of[6], 71), 0)
    return dict(layer_input=layer_input, query_preact=query_preact, key_preact=key_preact, value_rows=value_rows, output_grad=output_grad, log_decay=log_decay)


precise = lax.Precision.HIGHEST


def silu_slope(preact):
    sigmoid = jax.nn.sigmoid(preact)
    return sigmoid * (1.0 + preact * (1.0 - sigmoid))


def decay_mask(cumulative):
    length = cumulative.shape[1]
    causal = lax.broadcasted_iota(jnp.int32, (length, length), 0) >= lax.broadcasted_iota(jnp.int32, (length, length), 1)
    spread = cumulative[:, :, None] - cumulative[:, None, :]
    return jnp.where(causal[None], jnp.exp(jnp.minimum(spread, 0.0)), 0.0)


def block_forward(carried, blocks):
    queries, key_rows, value_rows, grad_rows, decay_rows = blocks
    queries32 = queries.astype(jnp.float32)
    keys32 = key_rows.astype(jnp.float32)
    values32 = value_rows.astype(jnp.float32)
    grads32 = grad_rows.astype(jnp.float32)
    cumulative = jnp.cumsum(decay_rows, axis=0).T
    weights = decay_mask(cumulative)
    scores_out = (jnp.einsum("thd,shd->hts", grads32, values32) * weights).astype(jnp.bfloat16).astype(jnp.float32)
    scores_in = (jnp.einsum("thd,shd->hts", queries32, keys32) * weights).astype(jnp.bfloat16).astype(jnp.float32)
    grad_query = jnp.einsum("hts,shd->thd", scores_out, keys32)
    grad_query = grad_query + jnp.exp(cumulative).T[:, :, None] * jnp.einsum("thj,hij->thi", grads32, carried, precision=precise)
    grad_key = jnp.einsum("hts,thd->shd", scores_out, queries32)
    grad_value = jnp.einsum("hts,thd->shd", scores_in, grads32)
    final_log = cumulative[:, -1]
    to_end = jnp.exp(final_log[:, None] - cumulative).T[:, :, None]
    updated = jnp.exp(final_log)[:, None, None] * carried + jnp.einsum("shi,shj->hij", keys32 * to_end, values32, precision=precise)
    return updated, (grad_query, grad_key, grad_value)


def block_backward(carried, blocks):
    queries, key_rows, value_rows, grad_rows, decay_rows, grad_key, grad_value = blocks
    cumulative = jnp.cumsum(decay_rows, axis=0).T
    final_log = cumulative[:, -1]
    to_end = jnp.exp(final_log[:, None] - cumulative).T[:, :, None]
    key_total = grad_key + to_end * jnp.einsum("thj,hij->thi", value_rows.astype(jnp.float32), carried, precision=precise)
    value_total = grad_value + to_end * jnp.einsum("thi,hij->thj", key_rows.astype(jnp.float32), carried, precision=precise)
    from_start = jnp.exp(cumulative).T[:, :, None]
    updated = jnp.exp(final_log)[:, None, None] * carried + jnp.einsum("thi,thj->hij", queries.astype(jnp.float32) * from_start, grad_rows.astype(jnp.float32), precision=precise)
    return updated, (key_total, value_total)


def reference(layer_input, query_preact, key_preact, value_rows, output_grad, log_decay):
    scaling = HEAD_DIM ** -0.5
    queries = (jax.nn.silu(query_preact.astype(jnp.float32)) * scaling).astype(jnp.bfloat16)
    key_rows = jax.nn.silu(key_preact.astype(jnp.float32)).astype(jnp.bfloat16)
    block_count = TOKEN_COUNT // BLOCK
    columns = HEAD_COUNT * HEAD_DIM

    def blocked(source_array):
        return source_array.reshape(block_count, BLOCK, HEAD_COUNT, HEAD_DIM)

    inputs_all = (blocked(queries), blocked(key_rows), blocked(value_rows), blocked(output_grad), log_decay.reshape(block_count, BLOCK, HEAD_COUNT))
    empty_state = jnp.zeros((HEAD_COUNT, HEAD_DIM, HEAD_DIM), jnp.float32)
    carried, (grad_query, grad_key, grad_value) = lax.scan(block_forward, empty_state, inputs_all)
    carried, (key_total, value_total) = lax.scan(block_backward, empty_state, inputs_all + (grad_key, grad_value), reverse=True)
    query_slope = (grad_query.reshape(TOKEN_COUNT, columns) * scaling * silu_slope(query_preact.astype(jnp.float32))).astype(jnp.bfloat16)
    key_slope = (key_total.reshape(TOKEN_COUNT, columns) * silu_slope(key_preact.astype(jnp.float32))).astype(jnp.bfloat16)
    value_grad = value_total.reshape(TOKEN_COUNT, columns).astype(jnp.bfloat16)
    slopes = jnp.concatenate([query_slope, key_slope], axis=1).reshape(N_SEQ, TOK_DEV, 2 * columns)
    grouped = layer_input.reshape(N_SEQ, TOK_DEV, D)

    def accumulate(running, pieces):
        partial_term = jnp.dot(pieces[0].astype(jnp.float32).T, pieces[1].astype(jnp.float32))
        rounded = lax.optimization_barrier(partial_term.astype(jnp.bfloat16)).astype(jnp.float32)
        return running + rounded, None

    running, unused = lax.scan(accumulate, jnp.zeros((D, 2 * columns), jnp.float32), (grouped, slopes))
    return running[:, :columns], running[:, columns:], value_grad
```

```python
import jax
import jax.numpy as jnp
import numpy as np
from jax import lax
from jax.experimental import pallas as pl
from jax.experimental.pallas import tpu as pltpu
from jax.sharding import Mesh, PartitionSpec as P

HEAD = 128
N_Y = 4
N_Z = 8
SEQ = N_Y * N_Z
CORES = 2
RANKS = CORES * SEQ
STEPS = 5
AXES = ("core", "y", "z")
MESSAGE = 48
BF16 = jnp.bfloat16
F32 = jnp.float32
VMEM = pltpu.CompilerParams(vmem_limit_bytes=48 * 2**20)


def exchange_plan(stream):
    by_z = [("z", 1, stream), ("y", 1, stream), ("z", 2, 2 * stream), ("y", 2, 0), ("z", 4, 0)]
    by_y = [("y", 1, stream), ("z", 1, stream), ("y", 2, 0), ("z", 2, 2 * stream), ("z", 4, 0)]
    return by_z, by_y


def rank_of(core, y, z):
    return (core * N_Y + y) * N_Z + z


def partner_of(kind, core, y, z):
    axis, distance, offset = kind
    if axis == "z":
        return rank_of(core, y, (((z - offset) ^ distance) + offset) % N_Z)
    return rank_of(core, (((y - offset) ^ distance) + offset) % N_Y, z)


def exchange_partners(stream):
    plan = exchange_plan(stream)
    steps = []
    for step in range(STEPS):
        partners = {}
        for core in range(CORES):
            for y in range(N_Y):
                for z in range(N_Z):
                    partners[rank_of(core, y, z)] = partner_of(plan[core][step], core, y, z)
        steps.append(partners)
    return steps


def block_order(stream):
    steps = exchange_partners(stream)
    order = {rank: [rank % SEQ] for rank in range(RANKS)}
    for partners in reversed(steps):
        order = {rank: order[rank] + order[partners[rank]] for rank in range(RANKS)}
    for rank in range(RANKS):
        assert sorted(order[rank]) == list(range(SEQ))
    return np.array([order[rank] for rank in range(RANKS)], np.int32)


PARTNERS = [exchange_partners(stream) for stream in range(2)]
ORDERS = np.stack([block_order(stream) for stream in range(2)])


def dot(a, b, contract):
    return lax.dot_general(a, b, ((contract[:1], contract[1:]), ((), ())), preferred_element_type=F32)


def split3(value):
    high = value.astype(BF16)
    rest = value - high.astype(F32)
    middle = rest.astype(BF16)
    low = (rest - middle.astype(F32)).astype(BF16)
    return high, middle, low


def states_kernel(query_ref, key_ref, value_ref, grad_ref, decay_ref, q_ref, k_ref, cum_ref, row_ref, out_ref):
    tokens, heads = decay_ref.shape
    scaling = HEAD ** (-0.5)
    x = query_ref[...].astype(F32)
    q_ref[...] = (x * jax.nn.sigmoid(x) * scaling).astype(BF16)
    x = key_ref[...].astype(F32)
    k_ref[...] = (x * jax.nn.sigmoid(x)).astype(BF16)
    rows = lax.broadcasted_iota(jnp.int32, (tokens, tokens), 0)
    columns = lax.broadcasted_iota(jnp.int32, (tokens, tokens), 1)
    lower = jnp.where(rows >= columns, 1.0, 0.0).astype(BF16)
    pieces = split3(decay_ref[...])
    cumulative = sum(dot(lower, piece, (1, 0)) for piece in pieces)
    across = sum(dot(piece, lower, (0, 1)) for piece in pieces)
    cum_ref[...] = cumulative
    row_ref[...] = across
    total = cumulative[tokens - 1 :, :]
    from_start = jnp.exp(cumulative)
    to_end = jnp.exp(total - cumulative)
    per = SEQ // (2 * heads)
    span = HEAD // per
    for head in range(heads):
        part = slice(head * HEAD, (head + 1) * HEAD)
        weighted_key = (k_ref[:, part].astype(F32) * to_end[:, head : head + 1]).astype(BF16)
        weighted_query = (q_ref[:, part].astype(F32) * from_start[:, head : head + 1]).astype(BF16)
        forward = dot(weighted_key, value_ref[:, part], (0, 0)).astype(BF16)
        backward = dot(weighted_query, grad_ref[:, part], (0, 0)).astype(BF16)
        marks = split3(jnp.broadcast_to(total[:, head : head + 1], (16, HEAD)))
        line = lax.broadcasted_iota(jnp.int32, (16, HEAD), 0)
        tail = jnp.where(line == 0, marks[0].astype(F32), jnp.where(line == 1, marks[1].astype(F32), marks[2].astype(F32)))
        tail = jnp.where(line < 3, tail, 0.0).astype(BF16)
        for direction, state in enumerate((forward, backward)):
            for piece in range(per):
                owner = (direction * heads + head) * per + piece
                out_ref[owner, :span, :] = state[piece * span : (piece + 1) * span, :]
                out_ref[owner, span:, :] = tail


def scan_kernel(place_ref, in_ref, out_ref):
    count = in_ref.shape[0]
    span = out_ref.shape[1]
    backward = place_ref[0] >= count // 2

    def step(at, carried):
        source = jnp.where(backward, count - 1 - at, at)
        out_ref[source] = carried.astype(BF16)
        message = in_ref[source].astype(F32)
        total = message[span : span + 1] + message[span + 1 : span + 2] + message[span + 2 : span + 3]
        return jnp.exp(total) * carried + message[:span]

    lax.fori_loop(0, count, step, jnp.zeros((span, HEAD), F32), unroll=4)


def silu_slope(value):
    sigmoid = jax.nn.sigmoid(value)
    return sigmoid * (1.0 + value * (1.0 - sigmoid))


def decay_weights(cum_ref, row_ref, head):
    tokens = cum_ref.shape[0]
    rows = lax.broadcasted_iota(jnp.int32, (tokens, tokens), 0)
    columns = lax.broadcasted_iota(jnp.int32, (tokens, tokens), 1)
    spread = cum_ref[:, head : head + 1] - row_ref[head : head + 1, :]
    return jnp.where(rows >= columns, jnp.exp(jnp.minimum(spread, 0.0)), 0.0)


def slopes_kernel(query_ref, key_ref, q_ref, k_ref, value_ref, grad_ref, cum_ref, row_ref, states_ref, qs_ref, ks_ref):
    tokens, heads = cum_ref.shape
    scaling = HEAD ** (-0.5)
    for head in range(heads):
        part = slice(head * HEAD, (head + 1) * HEAD)
        forward = states_ref[head * HEAD : (head + 1) * HEAD, :]
        backward = states_ref[(heads + head) * HEAD : (heads + head + 1) * HEAD, :]
        cumulative = cum_ref[:, head : head + 1]
        total = cum_ref[tokens - 1 :, head : head + 1]
        grads = grad_ref[:, part]
        values = value_ref[:, part]
        scores = (dot(grads, values, (1, 1)) * decay_weights(cum_ref, row_ref, head)).astype(BF16)
        grad_query = dot(scores, k_ref[:, part], (1, 0)) + jnp.exp(cumulative) * dot(grads, forward, (1, 1))
        qs_ref[:, part] = (grad_query * scaling * silu_slope(query_ref[:, part].astype(F32))).astype(BF16)
        grad_key = dot(scores, q_ref[:, part], (0, 0)) + jnp.exp(total - cumulative) * dot(values, backward, (1, 1))
        ks_ref[:, part] = (grad_key * silu_slope(key_ref[:, part].astype(F32))).astype(BF16)


def values_kernel(q_ref, k_ref, grad_ref, cum_ref, row_ref, states_ref, out_ref):
    tokens, heads = cum_ref.shape
    for head in range(heads):
        part = slice(head * HEAD, (head + 1) * HEAD)
        backward = states_ref[(heads + head) * HEAD : (heads + head + 1) * HEAD, :]
        cumulative = cum_ref[:, head : head + 1]
        total = cum_ref[tokens - 1 :, head : head + 1]
        keys = k_ref[:, part]
        scores = (dot(q_ref[:, part], keys, (1, 1)) * decay_weights(cum_ref, row_ref, head)).astype(BF16)
        grad_value = dot(scores, grad_ref[:, part], (0, 0)) + jnp.exp(total - cumulative) * dot(keys, backward, (1, 0))
        out_ref[:, part] = grad_value.astype(BF16)


def transpose_kernel(in_ref, out_ref):
    out_ref[...] = in_ref[...].T


def projection_kernel(order_ref, input_ref, slope_ref, out_ref, rows_ref):
    block = input_ref.shape[0] // SEQ
    blocks = out_ref.shape[0] // block
    for at in range(blocks):
        start = pl.multiple_of(order_ref[at] * block, block)
        rows_ref[at * block : (at + 1) * block, :] = input_ref[pl.ds(start, block), :]
    out_ref[...] = dot(rows_ref[...], slope_ref[...], (1, 0)).astype(out_ref.dtype)


def add_kernel(received_ref, kept_ref, keep_ref, send_ref):
    half = keep_ref.shape[0]
    keep_ref[...] = kept_ref[:half] + received_ref[:half].astype(F32)
    send_ref[...] = (kept_ref[half:] + received_ref[half:].astype(F32)).astype(BF16)


def last_add_kernel(received_ref, kept_ref, out_ref):
    out_ref[...] = kept_ref[...] + received_ref[...].astype(F32)


def shaped(shape, dtype):
    return jax.ShapeDtypeStruct(shape, dtype)


def cost(flops, moved):
    return pl.CostEstimate(flops=flops, bytes_accessed=moved, transcendentals=0)


def transposed(array):
    tokens, width = array.shape
    chunk = 384
    return pl.pallas_call(
        transpose_kernel,
        grid=(width // chunk,),
        in_specs=[pl.BlockSpec((tokens, chunk), lambda i: (0, i))],
        out_specs=pl.BlockSpec((chunk, tokens), lambda i: (i, 0)),
        out_shape=shaped((width, tokens), array.dtype),
        compiler_params=VMEM,
    )(array)


def projected(order, rows, slopes, dtype):
    width, tokens = rows.shape
    blocks = order.shape[0]
    taken = width // SEQ * blocks
    columns = slopes.shape[1]
    return pl.pallas_call(
        projection_kernel,
        in_specs=[pl.BlockSpec(memory_space=pltpu.SMEM)] + [pl.BlockSpec(memory_space=pltpu.VMEM)] * 2,
        out_specs=pl.BlockSpec(memory_space=pltpu.VMEM),
        out_shape=shaped((taken, columns), dtype),
        scratch_shapes=[pltpu.VMEM((taken, tokens), BF16)],
        compiler_params=VMEM,
        cost_estimate=cost(2 * taken * columns * tokens, 4 * taken * columns),
    )(order, rows, slopes)


def merged(received, kept):
    rows, columns = kept.shape
    half = rows // 2
    return pl.pallas_call(
        add_kernel,
        out_shape=(shaped((half, columns), F32), shaped((half, columns), BF16)),
        compiler_params=VMEM,
        cost_estimate=cost(rows * columns, 8 * rows * columns),
    )(received, kept)


def last_merged(received, kept):
    return pl.pallas_call(last_add_kernel, out_shape=shaped(kept.shape, F32), compiler_params=VMEM)(received, kept)


def per_device(layer_input, query_preact, key_preact, value_rows, output_grad, log_decay):
    tokens, heads = log_decay.shape
    columns = query_preact.shape[1]
    core, y, z = (lax.axis_index(axis) for axis in AXES)
    place = y * N_Z + z
    orders = jnp.asarray(ORDERS)[:, core * SEQ + place]
    half = SEQ // 2
    turned = transposed(layer_input)
    queries, key_rows, cumulative, across, states = pl.pallas_call(
        states_kernel,
        out_shape=(
            shaped((tokens, columns), BF16),
            shaped((tokens, columns), BF16),
            shaped((tokens, heads), F32),
            shaped((heads, tokens), F32),
            shaped((SEQ, MESSAGE, HEAD), BF16),
        ),
        compiler_params=VMEM,
    )(query_preact, key_preact, value_rows, output_grad, log_decay)
    states = lax.all_to_all(states, ("y", "z"), 0, 0, tiled=True)
    span = 2 * heads * HEAD // SEQ
    incoming = pl.pallas_call(
        scan_kernel,
        in_specs=[pl.BlockSpec(memory_space=pltpu.SMEM), pl.BlockSpec(memory_space=pltpu.VMEM)],
        out_specs=pl.BlockSpec(memory_space=pltpu.VMEM),
        out_shape=shaped((SEQ, span, HEAD), BF16),
        compiler_params=VMEM,
    )(place[None].astype(jnp.int32), states)
    incoming = lax.all_to_all(incoming, ("y", "z"), 0, 0, tiled=True).reshape(2 * heads * HEAD, HEAD)
    slopes = pl.pallas_call(
        slopes_kernel,
        out_shape=(shaped((tokens, columns), BF16), shaped((tokens, columns), BF16)),
        compiler_params=VMEM,
    )(query_preact, key_preact, queries, key_rows, value_rows, output_grad, cumulative, across, incoming)
    sends = [projected(orders[stream, half:], turned, slopes[stream], BF16) for stream in range(2)]
    keeps = [projected(orders[stream, :half], turned, slopes[stream], F32) for stream in range(2)]
    for step in range(STEPS):
        received = [
            lax.ppermute(sends[stream], AXES, sorted(PARTNERS[stream][step].items())) for stream in range(2)
        ]
        if step < STEPS - 1:
            pairs = [merged(received[stream], keeps[stream]) for stream in range(2)]
            keeps, sends = [pair[0] for pair in pairs], [pair[1] for pair in pairs]
        else:
            keeps = [last_merged(received[stream], keeps[stream]) for stream in range(2)]
    value_grad = pl.pallas_call(
        values_kernel,
        out_shape=shaped((tokens, columns), BF16),
        compiler_params=VMEM,
        cost_estimate=cost(2 * 3 * tokens * tokens * columns, 8 * tokens * columns),
    )(queries, key_rows, output_grad, cumulative, across, incoming)
    return keeps[0], keeps[1], value_grad


def solution(mesh):
    chips = mesh.devices.shape[0] // CORES
    split = Mesh(mesh.devices.reshape(chips, CORES, N_Y, N_Z), ("x",) + AXES)
    seq, cores = ("y", "z"), ("x", "core")
    both = P(seq, cores)
    return jax.shard_map(
        per_device,
        mesh=split,
        in_specs=(P(seq, None), both, both, both, both, both),
        out_specs=(both, both, both),
        check_vma=False,
    )
```

```python
import functools

import jax
import jax.numpy as jnp
import numpy as np
from jax import lax
from jax.experimental import pallas as pl
from jax.experimental.pallas import tpu as pltpu
from jax.sharding import Mesh, PartitionSpec as P

HEAD = 128
N_Y = 4
N_Z = 8
SEQ = N_Y * N_Z
CORES = 2
RANKS = CORES * SEQ
STEPS = 5
AXES = ("core", "y", "z")
MESSAGE = 48
BF16 = jnp.bfloat16
F32 = jnp.float32
VMEM = pltpu.CompilerParams(vmem_limit_bytes=20 * 2**20)
WIDE = pltpu.CompilerParams(vmem_limit_bytes=56 * 2**20)


def exchange_plan(stream, core):
    if stream == 0:
        return [("z", 1, core), ("y", 1, core), ("z", 2, 2 * core), ("y", 2, 0), ("z", 4, 0)]
    return [("y", 1, core), ("z", 1, core), ("y", 2, 0), ("z", 2, 2 * core), ("z", 4, 0)]


def rank_of(core, y, z):
    return (core * N_Y + y) * N_Z + z


def partner_of(kind, core, y, z):
    axis, distance, offset = kind
    if axis == "z":
        return rank_of(core, y, (((z - offset) ^ distance) + offset) % N_Z)
    return rank_of(core, (((y - offset) ^ distance) + offset) % N_Y, z)


def exchange_partners(stream):
    steps = []
    for step in range(STEPS):
        partners = {}
        for core in range(CORES):
            for y in range(N_Y):
                for z in range(N_Z):
                    partners[rank_of(core, y, z)] = partner_of(exchange_plan(stream, core)[step], core, y, z)
        steps.append(partners)
    return steps


def block_order(stream):
    steps = exchange_partners(stream)
    order = {rank: [rank % SEQ] for rank in range(RANKS)}
    for partners in reversed(steps):
        order = {rank: order[rank] + order[partners[rank]] for rank in range(RANKS)}
    for rank in range(RANKS):
        assert sorted(order[rank]) == list(range(SEQ))
    return np.array([order[rank] for rank in range(RANKS)], np.int32)


PARTNERS = [exchange_partners(stream) for stream in range(2)]
ORDERS = np.stack([block_order(stream) for stream in range(2)])


def dot(a, b, contract):
    return lax.dot_general(a, b, ((contract[:1], contract[1:]), ((), ())), preferred_element_type=F32)


def split3(value):
    high = value.astype(BF16)
    rest = value - high.astype(F32)
    middle = rest.astype(BF16)
    low = (rest - middle.astype(F32)).astype(BF16)
    return high, middle, low


def moves(sources, targets, semaphores, first=0):
    return [
        pltpu.make_async_copy(source, target, semaphores.at[first + at])
        for at, (source, target) in enumerate(zip(sources, targets))
    ]


def start_all(copies):
    for copy in copies:
        copy.start()


def prefix_sums(decay):
    tokens = decay.shape[1]
    rows = lax.broadcasted_iota(jnp.int32, (tokens, tokens), 0)
    columns = lax.broadcasted_iota(jnp.int32, (tokens, tokens), 1)
    lower = jnp.where(rows >= columns, 1.0, 0.0).astype(BF16)
    pieces = split3(decay)
    return sum(dot(lower, piece, (1, 1)) for piece in pieces), sum(dot(piece, lower, (1, 1)) for piece in pieces)


def states_kernel(
    decay_hbm, query_hbm, key_hbm, value_hbm, grad_hbm, out_ref,
    decay_ref, query_ref, key_ref, value_ref, grad_ref, semaphores,
):
    heads, tokens = decay_ref.shape
    scaling = HEAD ** (-0.5)
    copies = moves(
        (decay_hbm, key_hbm, value_hbm, query_hbm, grad_hbm),
        (decay_ref, key_ref, value_ref, query_ref, grad_ref),
        semaphores,
    )
    start_all(copies)
    copies[0].wait()
    cumulative, _ = prefix_sums(decay_ref[...])
    total = cumulative[tokens - 1 :, :]
    from_start = jnp.exp(cumulative)
    to_end = jnp.exp(total - cumulative)
    per = SEQ // (2 * heads)
    span = HEAD // per
    line = lax.broadcasted_iota(jnp.int32, (16, HEAD), 0)
    tails = []
    for head in range(heads):
        marks = split3(jnp.broadcast_to(total[:, head : head + 1], (16, HEAD)))
        tail = jnp.where(
            line == 0, marks[0].astype(F32), jnp.where(line == 1, marks[1].astype(F32), marks[2].astype(F32))
        )
        tails.append(jnp.where(line < 3, tail, 0.0).astype(BF16))

    def emit(direction, head, state):
        state = state.astype(BF16)
        for piece in range(per):
            owner = (direction * heads + head) * per + piece
            out_ref[owner, :span, :] = state[piece * span : (piece + 1) * span, :]
            out_ref[owner, span:, :] = tails[head]

    copies[1].wait()
    copies[2].wait()
    for head in range(heads):
        part = slice(head * HEAD, (head + 1) * HEAD)
        x = key_ref[:, part].astype(F32)
        keys = (x * jax.nn.sigmoid(x)).astype(BF16)
        weighted = (keys.astype(F32) * to_end[:, head : head + 1]).astype(BF16)
        emit(0, head, dot(weighted, value_ref[:, part], (0, 0)))
    copies[3].wait()
    copies[4].wait()
    for head in range(heads):
        part = slice(head * HEAD, (head + 1) * HEAD)
        x = query_ref[:, part].astype(F32)
        queries = (x * jax.nn.sigmoid(x) * scaling).astype(BF16)
        weighted = (queries.astype(F32) * from_start[:, head : head + 1]).astype(BF16)
        emit(1, head, dot(weighted, grad_ref[:, part], (0, 0)))


def scan_kernel(place_ref, in_ref, after_hbm, out_ref):
    count = in_ref.shape[0]
    span = out_ref.shape[1]
    backward = place_ref[0] >= count // 2

    def step(at, carried):
        source = jnp.where(backward, count - 1 - at, at)
        out_ref[source] = carried.astype(BF16)
        message = in_ref[source].astype(F32)
        total = message[span : span + 1] + message[span + 1 : span + 2] + message[span + 2 : span + 3]
        return jnp.exp(total) * carried + message[:span]

    lax.fori_loop(0, count, step, jnp.zeros((span, HEAD), F32), unroll=4)


def local_kernel(
    decay_hbm, query_hbm, key_hbm, value_hbm, grad_hbm,
    gq_hbm, gk_hbm, gv_hbm, sq_hbm, sk_hbm, wo_hbm, wv_hbm, wk_hbm,
    decay_ref, query_ref, key_ref, value_ref, grad_ref,
    q_ref, k_ref, gq_ref, gk_ref, gv_ref, sq_ref, sk_ref, wo_ref, wv_ref, wk_ref, cum_ref, row_ref, semaphores,
):
    heads, tokens = decay_ref.shape
    scaling = HEAD ** (-0.5)
    copies = moves(
        (decay_hbm, query_hbm, key_hbm, value_hbm, grad_hbm),
        (decay_ref, query_ref, key_ref, value_ref, grad_ref),
        semaphores,
    )
    start_all(copies)
    writes = moves(
        (gq_ref, gk_ref, gv_ref, sq_ref, sk_ref, wo_ref, wv_ref, wk_ref),
        (gq_hbm, gk_hbm, gv_hbm, sq_hbm, sk_hbm, wo_hbm, wv_hbm, wk_hbm),
        semaphores,
        len(copies),
    )
    copies[0].wait()
    cum_ref[...], row_ref[...] = prefix_sums(decay_ref[...])
    for copy in copies[1:]:
        copy.wait()
    half = tokens // 2
    rows = lax.broadcasted_iota(jnp.int32, (half, half), 0)
    columns = lax.broadcasted_iota(jnp.int32, (half, half), 1)
    causal = rows >= columns
    for head in range(heads):
        part = slice(head * HEAD, (head + 1) * HEAD)
        line = slice(head, head + 1)
        x = query_ref[:, part].astype(F32)
        sigmoid = jax.nn.sigmoid(x)
        q_ref[:, part] = (x * sigmoid * scaling).astype(BF16)
        sq_ref[:, part] = (sigmoid * (1.0 + x * (1.0 - sigmoid)) * scaling).astype(BF16)
        x = key_ref[:, part].astype(F32)
        sigmoid = jax.nn.sigmoid(x)
        keys = (x * sigmoid).astype(BF16)
        k_ref[:, part] = keys
        sk_ref[:, part] = (sigmoid * (1.0 + x * (1.0 - sigmoid))).astype(BF16)
        cumulative = cum_ref[:, line]
        to_end = jnp.exp(cum_ref[tokens - 1 :, line] - cumulative)
        wo_ref[:, part] = (jnp.exp(cumulative) * grad_ref[:, part].astype(F32)).astype(BF16)
        wv_ref[:, part] = (to_end * value_ref[:, part].astype(F32)).astype(BF16)
        wk_ref[:, part] = (to_end * keys.astype(F32)).astype(BF16)

        def diagonal(block):
            spread = cum_ref[block, line] - row_ref[line, block]
            return jnp.where(causal, jnp.exp(jnp.minimum(spread, 0.0)), 0.0)

        early, late = slice(0, half), slice(half, tokens)
        border = cum_ref[half - 1 : half, line]
        decay_first = diagonal(early)
        decay_last = diagonal(late)
        decay_rows = jnp.exp(jnp.minimum(cum_ref[late, line] - border, 0.0))
        decay_columns = jnp.exp(jnp.minimum(border - row_ref[line, early], 0.0))

        def scores(left, right):
            first = (dot(left[early, part], right[early, part], (1, 1)) * decay_first).astype(BF16)
            across = (dot(left[late, part], right[early, part], (1, 1)) * decay_rows * decay_columns).astype(BF16)
            last = (dot(left[late, part], right[late, part], (1, 1)) * decay_last).astype(BF16)
            return first, across, last

        first, across, last = scores(grad_ref, value_ref)
        gq_ref[early, part] = dot(first, k_ref[early, part], (1, 0)).astype(BF16)
        gq_ref[late, part] = (dot(across, k_ref[early, part], (1, 0)) + dot(last, k_ref[late, part], (1, 0))).astype(BF16)
        gk_ref[early, part] = (dot(first, q_ref[early, part], (0, 0)) + dot(across, q_ref[late, part], (0, 0))).astype(BF16)
        gk_ref[late, part] = dot(last, q_ref[late, part], (0, 0)).astype(BF16)
        first, across, last = scores(q_ref, k_ref)
        gv_ref[early, part] = dot(first, grad_ref[early, part], (0, 0)) + dot(across, grad_ref[late, part], (0, 0))
        gv_ref[late, part] = dot(last, grad_ref[late, part], (0, 0))
    start_all(writes)
    for copy in writes:
        copy.wait()


def heads_kernel(
    states_hbm, wo_hbm, gq_hbm, sq_hbm, wv_hbm, gk_hbm, sk_hbm,
    slopes_q_ref, slopes_k_ref,
    states_ref, wo_ref, gq_ref, sq_ref, wv_ref, gk_ref, sk_ref, semaphores,
):
    heads = wo_ref.shape[1] // HEAD
    copies = moves(
        (states_hbm, wo_hbm, gq_hbm, sq_hbm, wv_hbm, gk_hbm, sk_hbm),
        (states_ref, wo_ref, gq_ref, sq_ref, wv_ref, gk_ref, sk_ref),
        semaphores,
    )
    start_all(copies)
    for stream, (weighted, local, slope, slopes) in enumerate(
        ((wo_ref, gq_ref, sq_ref, slopes_q_ref), (wv_ref, gk_ref, sk_ref, slopes_k_ref))
    ):
        for copy in copies[1 + 3 * stream : 4 + 3 * stream] + copies[: 1 - stream]:
            copy.wait()
        for head in range(heads):
            part = slice(head * HEAD, (head + 1) * HEAD)
            state = slice((stream * heads + head) * HEAD, (stream * heads + head + 1) * HEAD)
            gradient = local[:, part].astype(F32) + dot(weighted[:, part], states_ref[state, :], (1, 1))
            slopes[:, part] = (gradient * slope[:, part].astype(F32)).astype(BF16)


def pair_kernel(
    own0_ref, rows0_ref, slopes0_ref, own1_ref, rows1_ref, slopes1_ref, keep0_ref, send0_ref, keep1_ref, send1_ref
):
    half = keep0_ref.shape[0]
    for own, rows, slopes, keep, send in (
        (own0_ref, rows0_ref, slopes0_ref, keep0_ref, send0_ref),
        (own1_ref, rows1_ref, slopes1_ref, keep1_ref, send1_ref),
    ):
        send[...] = (own[half:] + dot(rows[half:], slopes[...], (1, 0))).astype(BF16)
        keep[...] = own[:half] + dot(rows[:half], slopes[...], (1, 0))


def values_kernel(local_ref, weighted_ref, states_ref, out_ref):
    heads = out_ref.shape[1] // HEAD
    for head in range(heads):
        part = slice(head * HEAD, (head + 1) * HEAD)
        later = slice((heads + head) * HEAD, (heads + head + 1) * HEAD)
        out_ref[:, part] = (local_ref[:, part] + dot(weighted_ref[:, part], states_ref[later, :], (1, 0))).astype(BF16)


def arrange_kernel(place_ref, table_ref, input_hbm, *refs, first):
    out0_hbm, out1_hbm, input_ref, turned_ref, out0_ref, out1_ref, semaphores = refs[-7:]
    tokens, width = input_ref.shape
    block = width // SEQ
    chunk = 384
    reads = moves(
        [input_hbm.at[:, at : at + chunk] for at in range(0, width, chunk)],
        [input_ref.at[:, at : at + chunk] for at in range(0, width, chunk)],
        semaphores,
    )
    start_all(reads)
    writes = moves((out0_ref, out1_ref), (out0_hbm, out1_hbm), semaphores, len(reads))
    for at, copy in enumerate(reads):
        copy.wait()
        turned_ref[at * chunk : (at + 1) * chunk, :] = input_ref[:, at * chunk : (at + 1) * chunk].T
    for stream, target in enumerate((out0_ref, out1_ref)):
        for at in range(SEQ // 2):
            entry = (stream * RANKS + place_ref[0]) * SEQ + first + at
            start = pl.multiple_of(table_ref[entry] * block, block)
            target[at * block : (at + 1) * block, :] = turned_ref[pl.ds(start, block), :]
        writes[stream].start()
    for copy in writes:
        copy.wait()


def projection_kernel(rows_ref, slope_ref, out_ref):
    out_ref[...] = dot(rows_ref[...], slope_ref[...], (1, 0))


def add_kernel(received0_ref, kept0_ref, received1_ref, kept1_ref, keep0_ref, send0_ref, keep1_ref, send1_ref):
    half = keep0_ref.shape[0]
    for received, kept, keep, send in (
        (received0_ref, kept0_ref, keep0_ref, send0_ref),
        (received1_ref, kept1_ref, keep1_ref, send1_ref),
    ):
        keep[...] = kept[:half] + received[:half].astype(F32)
        send[...] = (kept[half:] + received[half:].astype(F32)).astype(BF16)


def join_kernel(received0_ref, kept0_ref, received1_ref, kept1_ref, keep_ref, send_ref):
    half, columns = keep_ref.shape[0], kept0_ref.shape[1]
    for stream, (received, kept) in enumerate(((received0_ref, kept0_ref), (received1_ref, kept1_ref))):
        part = slice(stream * columns, (stream + 1) * columns)
        keep_ref[:, part] = kept[:half] + received[:half].astype(F32)
        send_ref[:, part] = (kept[half:] + received[half:].astype(F32)).astype(BF16)


def last_kernel(received_ref, kept_ref, out0_ref, out1_ref):
    columns = out0_ref.shape[1]
    for stream, out in enumerate((out0_ref, out1_ref)):
        part = slice(stream * columns, (stream + 1) * columns)
        out[...] = kept_ref[:, part] + received_ref[:, part].astype(F32)


def shaped(shape, dtype):
    return jax.ShapeDtypeStruct(shape, dtype)


def cost(flops, moved):
    return pl.CostEstimate(flops=flops, bytes_accessed=moved, transcendentals=0)


IN_HBM = pl.BlockSpec(memory_space=pltpu.HBM)
IN_VMEM = pl.BlockSpec(memory_space=pltpu.VMEM)


def per_device(layer_input, query_preact, key_preact, value_rows, output_grad, log_decay):
    tokens, heads = log_decay.shape
    columns = query_preact.shape[1]
    width = layer_input.shape[1]
    core, y, z = (lax.axis_index(axis) for axis in AXES)
    place = y * N_Z + z
    half = width // 2
    small, large = shaped((tokens, columns), BF16), shaped((tokens, columns), F32)
    partial = shaped((half, columns), BF16)
    turned = shaped((half, tokens), BF16)
    decay = shaped((heads, tokens), F32)
    states_shape = shaped((2 * heads * HEAD, HEAD), BF16)
    arguments = (log_decay.T, query_preact, key_preact, value_rows, output_grad)

    def scratch(*shapes):
        return [pltpu.VMEM(one.shape, one.dtype) for one in shapes]

    def semaphores(count):
        return [pltpu.SemaphoreType.DMA((count,))]

    states = pl.pallas_call(
        states_kernel,
        in_specs=[IN_HBM] * 5,
        out_shape=shaped((SEQ, MESSAGE, HEAD), BF16),
        scratch_shapes=scratch(decay, small, small, small, small) + semaphores(5),
        compiler_params=WIDE,
        cost_estimate=cost(10**9, 4 * 10**6),
    )(*arguments)
    states = lax.all_to_all(states, ("y", "z"), 0, 0, tiled=True)
    local_shapes = (small, small, large, small, small, small, small, small)
    local_q, local_k, local_v, slope_q, slope_k, weighted_o, weighted_v, weighted_k = pl.pallas_call(
        local_kernel,
        in_specs=[IN_HBM] * 5,
        out_specs=(IN_HBM,) * 8,
        out_shape=local_shapes,
        scratch_shapes=scratch(decay, *(small,) * 6, *local_shapes, shaped((tokens, heads), F32), decay)
        + semaphores(13),
        compiler_params=WIDE,
        cost_estimate=cost(4 * 10**9, 10**7),
    )(*arguments)
    rank = (core * SEQ + place)[None].astype(jnp.int32)
    table = jnp.asarray(ORDERS.reshape(-1))
    chunks = width // 384

    def arranged(first, *after):
        return pl.pallas_call(
            functools.partial(arrange_kernel, first=first),
            in_specs=[pl.BlockSpec(memory_space=pltpu.SMEM)] * 2 + [IN_HBM] + [pl.BlockSpec(memory_space=pl.ANY)] * len(after),
            out_specs=(IN_HBM,) * 2,
            out_shape=(turned,) * 2,
            scratch_shapes=scratch(shaped((tokens, width), BF16), shaped((width, tokens), BF16), turned, turned)
            + semaphores(chunks + 2),
            compiler_params=WIDE,
            cost_estimate=cost(10**9, 10**7),
        )(rank, table, layer_input, *after)

    sent0, sent1 = arranged(SEQ // 2)
    span = 2 * heads * HEAD // SEQ
    incoming = pl.pallas_call(
        scan_kernel,
        in_specs=[pl.BlockSpec(memory_space=pltpu.SMEM), IN_VMEM, IN_HBM],
        out_shape=shaped((SEQ, span, HEAD), BF16),
        compiler_params=VMEM,
    )(place[None].astype(jnp.int32), states, sent0)
    incoming = lax.all_to_all(incoming, ("y", "z"), 0, 0, tiled=True).reshape(2 * heads * HEAD, HEAD)
    flops = 2 * half * columns * tokens

    def exchange(stream, step, array):
        return lax.ppermute(array, AXES, sorted(PARTNERS[stream][step].items()))

    other0, other1 = exchange(0, 0, sent0), exchange(1, 0, sent1)
    slopes_q, slopes_k = pl.pallas_call(
        heads_kernel,
        in_specs=[pl.BlockSpec(memory_space=pl.ANY)] + [IN_HBM] * 6,
        out_shape=(small, small),
        scratch_shapes=scratch(states_shape, *(small,) * 6) + semaphores(7),
        compiler_params=WIDE,
        cost_estimate=cost(10**9, 4 * 10**6),
    )(incoming, weighted_o, local_q, slope_q, weighted_v, local_k, slope_k)
    partner_q, partner_k = exchange(0, 0, slopes_q), exchange(1, 0, slopes_k)
    kept0, kept1 = arranged(0, slopes_q)
    keeps = [
        pl.pallas_call(
            projection_kernel,
            out_shape=shaped((half, columns), F32),
            compiler_params=VMEM,
            cost_estimate=cost(flops, 5 * 10**6),
        )(rows, slopes)
        for rows, slopes in ((kept0, slopes_q), (kept1, slopes_k))
    ]
    rows = half // 2
    pair = (shaped((rows, columns), F32), shaped((rows, columns), BF16))
    keep0, send0, keep1, send1 = pl.pallas_call(
        pair_kernel, out_shape=pair + pair, compiler_params=VMEM, cost_estimate=cost(2 * flops, 12 * 10**6)
    )(keeps[0], other0, partner_q, keeps[1], other1, partner_k)
    for step in range(1, STEPS - 1):
        operands = (exchange(0, step, send0), keep0, exchange(1, step, send1), keep1)
        rows //= 2
        if step < STEPS - 2:
            pair = (shaped((rows, columns), F32), shaped((rows, columns), BF16))
            keep0, send0, keep1, send1 = pl.pallas_call(
                add_kernel, out_shape=pair + pair, compiler_params=VMEM
            )(*operands)
        else:
            keep, send = pl.pallas_call(
                join_kernel,
                out_shape=(shaped((rows, 2 * columns), F32), shaped((rows, 2 * columns), BF16)),
                compiler_params=VMEM,
            )(*operands)
    assert PARTNERS[0][STEPS - 1] == PARTNERS[1][STEPS - 1]
    received = exchange(0, STEPS - 1, send)
    qweight_grad, kweight_grad = pl.pallas_call(
        last_kernel, out_shape=(shaped((rows, columns), F32),) * 2, compiler_params=VMEM
    )(received, keep)
    value_grad = pl.pallas_call(
        values_kernel,
        out_shape=small,
        compiler_params=VMEM,
        cost_estimate=cost(10**9, 5 * 10**6),
    )(local_v, weighted_k, incoming)
    return qweight_grad, kweight_grad, value_grad


def solution(mesh):
    chips = mesh.devices.shape[0] // CORES
    split = Mesh(mesh.devices.reshape(chips, CORES, N_Y, N_Z), ("x",) + AXES)
    seq, cores = ("y", "z"), ("x", "core")
    both = P(seq, cores)
    return jax.shard_map(
        per_device,
        mesh=split,
        in_specs=(P(seq, None), both, both, both, both, both),
        out_specs=(both, both, both),
        check_vma=False,
    )
```

```python
import functools

import jax
import jax.numpy as jnp
import numpy as np
from jax import lax
from jax.experimental import pallas as pl
from jax.experimental.pallas import tpu as pltpu
from jax.sharding import Mesh, PartitionSpec as P

HEAD = 128
N_Y = 4
N_Z = 8
SEQ = N_Y * N_Z
CORES = 2
RANKS = CORES * SEQ
STEPS = 5
AXES = ("core", "y", "z")
MESSAGE = 40
BF16 = jnp.bfloat16
F32 = jnp.float32
VMEM = pltpu.CompilerParams(vmem_limit_bytes=20 * 2**20)
WIDE = pltpu.CompilerParams(vmem_limit_bytes=56 * 2**20)


def exchange_plan(stream, core):
    if stream == 0:
        return [("z", 1, core), ("y", 1, core), ("z", 2, 2 * core), ("y", 2, 0), ("z", 4, 0)]
    return [("y", 1, core), ("z", 1, core), ("y", 2, 0), ("z", 2, 2 * core), ("z", 4, 0)]


def rank_of(core, y, z):
    return (core * N_Y + y) * N_Z + z


def partner_of(kind, core, y, z):
    axis, distance, offset = kind
    if axis == "z":
        return rank_of(core, y, (((z - offset) ^ distance) + offset) % N_Z)
    return rank_of(core, (((y - offset) ^ distance) + offset) % N_Y, z)


def exchange_partners(stream):
    steps = []
    for step in range(STEPS):
        partners = {}
        for core in range(CORES):
            for y in range(N_Y):
                for z in range(N_Z):
                    partners[rank_of(core, y, z)] = partner_of(exchange_plan(stream, core)[step], core, y, z)
        steps.append(partners)
    return steps


def block_order(stream):
    steps = exchange_partners(stream)
    order = {rank: [rank % SEQ] for rank in range(RANKS)}
    for partners in reversed(steps):
        order = {rank: order[rank] + order[partners[rank]] for rank in range(RANKS)}
    for rank in range(RANKS):
        assert sorted(order[rank]) == list(range(SEQ))
    return np.array([order[rank] for rank in range(RANKS)], np.int32)


PARTNERS = [exchange_partners(stream) for stream in range(2)]
ORDERS = np.stack([block_order(stream) for stream in range(2)])


def dot(a, b, contract):
    return lax.dot_general(a, b, ((contract[:1], contract[1:]), ((), ())), preferred_element_type=F32)


def split3(value):
    high = value.astype(BF16)
    rest = value - high.astype(F32)
    middle = rest.astype(BF16)
    low = (rest - middle.astype(F32)).astype(BF16)
    return high, middle, low


def moves(sources, targets, semaphores, first=0):
    return [
        pltpu.make_async_copy(source, target, semaphores.at[first + at])
        for at, (source, target) in enumerate(zip(sources, targets))
    ]


def start_all(copies):
    for copy in copies:
        copy.start()


def prefix_sums(decay):
    heads, tokens = decay.shape
    rows = lax.broadcasted_iota(jnp.int32, (tokens, tokens), 0)
    columns = lax.broadcasted_iota(jnp.int32, (tokens, tokens), 1)
    lower = jnp.where(rows >= columns, 1.0, 0.0).astype(BF16)
    parts = jnp.concatenate([piece.astype(F32) for piece in split3(decay)], axis=0).astype(BF16)
    down = dot(lower, parts, (1, 1))
    across = dot(parts, lower, (1, 1))
    return (
        down[:, :heads] + down[:, heads : 2 * heads] + down[:, 2 * heads :],
        across[:heads] + across[heads : 2 * heads] + across[2 * heads :],
    )


def states_kernel(
    decay_hbm, query_hbm, key_hbm, value_hbm, grad_hbm, out_ref,
    decay_ref, query_ref, key_ref, value_ref, grad_ref, semaphores,
):
    heads, tokens = decay_ref.shape
    scaling = HEAD ** (-0.5)
    copies = moves(
        (decay_hbm, key_hbm, value_hbm, query_hbm, grad_hbm),
        (decay_ref, key_ref, value_ref, query_ref, grad_ref),
        semaphores,
    )
    start_all(copies)
    copies[0].wait()
    cumulative, _ = prefix_sums(decay_ref[...])
    total = cumulative[tokens - 1 :, :]
    from_start = jnp.exp(cumulative)
    to_end = jnp.exp(total - cumulative)
    per = SEQ // (2 * heads)
    span = HEAD // per
    line = lax.broadcasted_iota(jnp.int32, (MESSAGE - span, HEAD), 0)
    tails = []
    for head in range(heads):
        marks = split3(jnp.broadcast_to(total[:, head : head + 1], (MESSAGE - span, HEAD)))
        tail = jnp.where(
            line == 0, marks[0].astype(F32), jnp.where(line == 1, marks[1].astype(F32), marks[2].astype(F32))
        )
        tails.append(jnp.where(line < 3, tail, 0.0).astype(BF16))

    def emit(direction, head, state):
        state = state.astype(BF16)
        for piece in range(per):
            owner = (direction * heads + head) * per + piece
            out_ref[owner, :span, :] = state[piece * span : (piece + 1) * span, :]
            out_ref[owner, span:, :] = tails[head]

    copies[1].wait()
    copies[2].wait()
    for head in range(heads):
        part = slice(head * HEAD, (head + 1) * HEAD)
        x = key_ref[:, part].astype(F32)
        keys = (x * jax.nn.sigmoid(x)).astype(BF16)
        weighted = (keys.astype(F32) * to_end[:, head : head + 1]).astype(BF16)
        emit(0, head, dot(weighted, value_ref[:, part], (0, 0)))
    copies[3].wait()
    copies[4].wait()
    for head in range(heads):
        part = slice(head * HEAD, (head + 1) * HEAD)
        x = query_ref[:, part].astype(F32)
        queries = (x * jax.nn.sigmoid(x) * scaling).astype(BF16)
        weighted = (queries.astype(F32) * from_start[:, head : head + 1]).astype(BF16)
        emit(1, head, dot(weighted, grad_ref[:, part], (0, 0)))


def scan_kernel(place_ref, in_ref, out_ref):
    count = in_ref.shape[0]
    span = out_ref.shape[1]
    backward = place_ref[0] >= count // 2

    def step(at, carried):
        source = jnp.where(backward, count - 1 - at, at)
        out_ref[source] = carried.astype(BF16)
        message = in_ref[source].astype(F32)
        total = message[span : span + 1] + message[span + 1 : span + 2] + message[span + 2 : span + 3]
        return jnp.exp(total) * carried + message[:span]

    lax.fori_loop(0, count, step, jnp.zeros((span, HEAD), F32), unroll=4)


def local_kernel(
    decay_hbm, query_hbm, key_hbm, value_hbm, grad_hbm,
    gq_hbm, gk_hbm, gv_hbm, sq_hbm, sk_hbm, wo_hbm, wv_hbm, wk_hbm,
    decay_ref, query_ref, key_ref, value_ref, grad_ref,
    q_ref, k_ref, gq_ref, gk_ref, gv_ref, sq_ref, sk_ref, wo_ref, wv_ref, wk_ref, cum_ref, row_ref, semaphores,
):
    heads, tokens = decay_ref.shape
    scaling = HEAD ** (-0.5)
    copies = moves(
        (decay_hbm, query_hbm, key_hbm, value_hbm, grad_hbm),
        (decay_ref, query_ref, key_ref, value_ref, grad_ref),
        semaphores,
    )
    start_all(copies)
    writes = moves(
        (gq_ref, gk_ref, gv_ref, sq_ref, sk_ref, wo_ref, wv_ref, wk_ref),
        (gq_hbm, gk_hbm, gv_hbm, sq_hbm, sk_hbm, wo_hbm, wv_hbm, wk_hbm),
        semaphores,
        len(copies),
    )
    copies[0].wait()
    cum_ref[...], row_ref[...] = prefix_sums(decay_ref[...])
    for copy in copies[1:]:
        copy.wait()
    half = tokens // 2
    rows = lax.broadcasted_iota(jnp.int32, (half, half), 0)
    columns = lax.broadcasted_iota(jnp.int32, (half, half), 1)
    causal = rows >= columns
    for head in range(heads):
        part = slice(head * HEAD, (head + 1) * HEAD)
        line = slice(head, head + 1)
        x = query_ref[:, part].astype(F32)
        sigmoid = jax.nn.sigmoid(x)
        q_ref[:, part] = (x * sigmoid * scaling).astype(BF16)
        sq_ref[:, part] = (sigmoid * (1.0 + x * (1.0 - sigmoid)) * scaling).astype(BF16)
        x = key_ref[:, part].astype(F32)
        sigmoid = jax.nn.sigmoid(x)
        keys = (x * sigmoid).astype(BF16)
        k_ref[:, part] = keys
        sk_ref[:, part] = (sigmoid * (1.0 + x * (1.0 - sigmoid))).astype(BF16)
        cumulative = cum_ref[:, line]
        to_end = jnp.exp(cum_ref[tokens - 1 :, line] - cumulative)
        wo_ref[:, part] = (jnp.exp(cumulative) * grad_ref[:, part].astype(F32)).astype(BF16)
        wv_ref[:, part] = (to_end * value_ref[:, part].astype(F32)).astype(BF16)
        wk_ref[:, part] = (to_end * keys.astype(F32)).astype(BF16)

        def diagonal(block):
            spread = cum_ref[block, line] - row_ref[line, block]
            return jnp.where(causal, jnp.exp(jnp.minimum(spread, 0.0)), 0.0)

        early, late = slice(0, half), slice(half, tokens)
        border = cum_ref[half - 1 : half, line]
        decay_first = diagonal(early)
        decay_last = diagonal(late)
        decay_rows = jnp.exp(jnp.minimum(cum_ref[late, line] - border, 0.0))
        decay_columns = jnp.exp(jnp.minimum(border - row_ref[line, early], 0.0))

        def scores(left, right):
            first = (dot(left[early, part], right[early, part], (1, 1)) * decay_first).astype(BF16)
            across = (dot(left[late, part], right[early, part], (1, 1)) * decay_rows * decay_columns).astype(BF16)
            last = (dot(left[late, part], right[late, part], (1, 1)) * decay_last).astype(BF16)
            return first, across, last

        first, across, last = scores(grad_ref, value_ref)
        gq_ref[early, part] = dot(first, k_ref[early, part], (1, 0)).astype(BF16)
        gq_ref[late, part] = (dot(across, k_ref[early, part], (1, 0)) + dot(last, k_ref[late, part], (1, 0))).astype(BF16)
        gk_ref[early, part] = (dot(first, q_ref[early, part], (0, 0)) + dot(across, q_ref[late, part], (0, 0))).astype(BF16)
        gk_ref[late, part] = dot(last, q_ref[late, part], (0, 0)).astype(BF16)
        first, across, last = scores(q_ref, k_ref)
        gv_ref[early, part] = dot(first, grad_ref[early, part], (0, 0)) + dot(across, grad_ref[late, part], (0, 0))
        gv_ref[late, part] = dot(last, grad_ref[late, part], (0, 0))
    start_all(writes)
    for copy in writes:
        copy.wait()


def heads_kernel(
    states_hbm, wo_hbm, gq_hbm, sq_hbm, wv_hbm, gk_hbm, sk_hbm,
    slopes_q_ref, slopes_k_ref,
    states_ref, wo_ref, gq_ref, sq_ref, wv_ref, gk_ref, sk_ref, semaphores,
):
    heads = wo_ref.shape[1] // HEAD
    copies = moves(
        (wo_hbm, states_hbm, gq_hbm, sq_hbm, wv_hbm, gk_hbm, sk_hbm),
        (wo_ref, states_ref, gq_ref, sq_ref, wv_ref, gk_ref, sk_ref),
        semaphores,
    )
    start_all(copies)
    for stream, (weighted, local, slope, slopes) in enumerate(
        ((wo_ref, gq_ref, sq_ref, slopes_q_ref), (wv_ref, gk_ref, sk_ref, slopes_k_ref))
    ):
        for copy in copies[4 * stream : 4 * stream + 4 - stream]:
            copy.wait()
        for head in range(heads):
            part = slice(head * HEAD, (head + 1) * HEAD)
            state = slice((stream * heads + head) * HEAD, (stream * heads + head + 1) * HEAD)
            gradient = local[:, part].astype(F32) + dot(weighted[:, part], states_ref[state, :], (1, 1))
            slopes[:, part] = (gradient * slope[:, part].astype(F32)).astype(BF16)


def pair_kernel(own0_ref, rows0_ref, slopes0_ref, own1_ref, rows1_ref, slopes1_ref, *refs, first):
    out0_ref, out1_ref = refs[-2:]
    part = slice(first, first + out0_ref.shape[0])
    for own, rows, slopes, out in (
        (own0_ref, rows0_ref, slopes0_ref, out0_ref),
        (own1_ref, rows1_ref, slopes1_ref, out1_ref),
    ):
        out[...] = (own[part] + dot(rows[...], slopes[...], (1, 0))).astype(out.dtype)


def values_kernel(local_ref, weighted_ref, states_ref, out_ref):
    heads = out_ref.shape[1] // HEAD
    for head in range(heads):
        part = slice(head * HEAD, (head + 1) * HEAD)
        later = slice((heads + head) * HEAD, (heads + head + 1) * HEAD)
        out_ref[:, part] = (local_ref[:, part] + dot(weighted_ref[:, part], states_ref[later, :], (1, 0))).astype(BF16)


def arrange_kernel(
    place_ref, table_ref, input_hbm,
    late0_hbm, late1_hbm, early0_hbm, early1_hbm, kept0_hbm, kept1_hbm,
    input_ref, turned_ref, late0_ref, late1_ref, early0_ref, early1_ref, kept0_ref, kept1_ref, semaphores,
):
    tokens, width = input_ref.shape
    block = width // SEQ
    chunk = 384
    reads = moves(
        [input_hbm.at[:, at : at + chunk] for at in range(0, width, chunk)],
        [input_ref.at[:, at : at + chunk] for at in range(0, width, chunk)],
        semaphores,
    )
    start_all(reads)
    outs = (late0_ref, late1_ref, early0_ref, early1_ref, kept0_ref, kept1_ref)
    targets = (late0_hbm, late1_hbm, early0_hbm, early1_hbm, kept0_hbm, kept1_hbm)
    writes = moves(outs, targets, semaphores, len(reads))
    for at, copy in enumerate(reads):
        copy.wait()
        turned_ref[at * chunk : (at + 1) * chunk, :] = input_ref[:, at * chunk : (at + 1) * chunk].T
    firsts = (3 * SEQ // 4, 3 * SEQ // 4, SEQ // 2, SEQ // 2, 0, 0)
    for out, write, stream, first in zip(outs, writes, (0, 1) * 3, firsts):
        for at in range(out.shape[0] // block):
            entry = (stream * RANKS + place_ref[0]) * SEQ + first + at
            start = pl.multiple_of(table_ref[entry] * block, block)
            out[at * block : (at + 1) * block, :] = turned_ref[pl.ds(start, block), :]
        write.start()
    for copy in writes:
        copy.wait()


def own_kernel(
    rows0_hbm, rows1_hbm, slopes0_ref, slopes1_ref, out0_ref, out1_ref, rows0_ref, rows1_ref, semaphores
):
    copies = moves((rows0_hbm, rows1_hbm), (rows0_ref, rows1_ref), semaphores)
    start_all(copies)
    for copy, rows, slopes, out in zip(
        copies, (rows0_ref, rows1_ref), (slopes0_ref, slopes1_ref), (out0_ref, out1_ref)
    ):
        copy.wait()
        out[...] = dot(rows[...], slopes[...], (1, 0))


def add_kernel(received0_ref, kept0_ref, received1_ref, kept1_ref, keep0_ref, send0_ref, keep1_ref, send1_ref):
    half = keep0_ref.shape[0]
    for received, kept, keep, send in (
        (received0_ref, kept0_ref, keep0_ref, send0_ref),
        (received1_ref, kept1_ref, keep1_ref, send1_ref),
    ):
        keep[...] = kept[:half] + received[:half].astype(F32)
        send[...] = (kept[half:] + received[half:].astype(F32)).astype(BF16)


def join_kernel(received0_ref, kept0_ref, received1_ref, kept1_ref, keep_ref, send_ref):
    half, columns = keep_ref.shape[0], kept0_ref.shape[1]
    for stream, (received, kept) in enumerate(((received0_ref, kept0_ref), (received1_ref, kept1_ref))):
        part = slice(stream * columns, (stream + 1) * columns)
        keep_ref[:, part] = kept[:half] + received[:half].astype(F32)
        send_ref[:, part] = (kept[half:] + received[half:].astype(F32)).astype(BF16)


def last_kernel(received_ref, kept_ref, out0_ref, out1_ref):
    columns = out0_ref.shape[1]
    for stream, out in enumerate((out0_ref, out1_ref)):
        part = slice(stream * columns, (stream + 1) * columns)
        out[...] = kept_ref[:, part] + received_ref[:, part].astype(F32)


def shaped(shape, dtype):
    return jax.ShapeDtypeStruct(shape, dtype)


def cost(flops, moved):
    return pl.CostEstimate(flops=flops, bytes_accessed=moved, transcendentals=0)


IN_HBM = pl.BlockSpec(memory_space=pltpu.HBM)
IN_VMEM = pl.BlockSpec(memory_space=pltpu.VMEM)


def per_device(layer_input, query_preact, key_preact, value_rows, output_grad, log_decay):
    tokens, heads = log_decay.shape
    columns = query_preact.shape[1]
    width = layer_input.shape[1]
    core, y, z = (lax.axis_index(axis) for axis in AXES)
    place = y * N_Z + z
    half = width // 2
    small, large = shaped((tokens, columns), BF16), shaped((tokens, columns), F32)
    partial = shaped((half, columns), BF16)
    turned = shaped((half, tokens), BF16)
    decay = shaped((heads, tokens), F32)
    states_shape = shaped((2 * heads * HEAD, HEAD), BF16)
    arguments = (log_decay.T, query_preact, key_preact, value_rows, output_grad)

    def scratch(*shapes):
        return [pltpu.VMEM(one.shape, one.dtype) for one in shapes]

    def semaphores(count):
        return [pltpu.SemaphoreType.DMA((count,))]

    states = pl.pallas_call(
        states_kernel,
        in_specs=[IN_HBM] * 5,
        out_shape=shaped((SEQ, MESSAGE, HEAD), BF16),
        scratch_shapes=scratch(decay, small, small, small, small) + semaphores(5),
        compiler_params=WIDE,
        cost_estimate=cost(10**9, 4 * 10**6),
    )(*arguments)
    states = lax.all_to_all(states, ("y", "z"), 0, 0, tiled=True)
    local_shapes = (small, small, large, small, small, small, small, small)
    local_q, local_k, local_v, slope_q, slope_k, weighted_o, weighted_v, weighted_k = pl.pallas_call(
        local_kernel,
        in_specs=[IN_HBM] * 5,
        out_specs=(IN_HBM,) * 8,
        out_shape=local_shapes,
        scratch_shapes=scratch(decay, *(small,) * 6, *local_shapes, shaped((tokens, heads), F32), decay)
        + semaphores(13),
        compiler_params=WIDE,
        cost_estimate=cost(6 * 10**10, 10**7),
    )(*arguments)
    rank = (core * SEQ + place)[None].astype(jnp.int32)
    table = jnp.asarray(ORDERS.reshape(-1))
    chunks = width // 384

    quarter = shaped((half // 2, tokens), BF16)
    arranged = (quarter,) * 4 + (turned,) * 2
    late0, late1, early0, early1, kept0, kept1 = pl.pallas_call(
        arrange_kernel,
        in_specs=[pl.BlockSpec(memory_space=pltpu.SMEM)] * 2 + [IN_HBM],
        out_specs=(IN_HBM,) * 6,
        out_shape=arranged,
        scratch_shapes=scratch(shaped((tokens, width), BF16), shaped((width, tokens), BF16), *arranged)
        + semaphores(chunks + 6),
        compiler_params=WIDE,
        cost_estimate=cost(10**9, 10**7),
    )(rank, table, layer_input)
    states, kept0 = lax.optimization_barrier((states, kept0))
    span = 2 * heads * HEAD // SEQ
    incoming = pl.pallas_call(
        scan_kernel,
        in_specs=[pl.BlockSpec(memory_space=pltpu.SMEM), IN_VMEM],
        out_shape=shaped((SEQ, span, HEAD), BF16),
        compiler_params=VMEM,
    )(place[None].astype(jnp.int32), states)
    incoming, early0, early1 = lax.optimization_barrier((incoming, early0, early1))
    incoming = lax.all_to_all(incoming, ("y", "z"), 0, 0, tiled=True).reshape(2 * heads * HEAD, HEAD)
    flops = 2 * half * columns * tokens

    def exchange(stream, step, array):
        return lax.ppermute(array, AXES, sorted(PARTNERS[stream][step].items()))

    late0, late1 = exchange(0, 0, late0), exchange(1, 0, late1)
    early0, early1 = exchange(0, 0, early0), exchange(1, 0, early1)
    early0, early1, kept0 = lax.optimization_barrier((early0, early1, kept0))
    slopes_q, slopes_k = pl.pallas_call(
        heads_kernel,
        in_specs=[pl.BlockSpec(memory_space=pl.ANY)] + [IN_HBM] * 6,
        out_shape=(small, small),
        scratch_shapes=scratch(states_shape, *(small,) * 6) + semaphores(7),
        compiler_params=WIDE,
        cost_estimate=cost(10**9, 4 * 10**6),
    )(incoming, weighted_o, local_q, slope_q, weighted_v, local_k, slope_k)
    partner_q, partner_k = exchange(0, 0, slopes_q), exchange(1, 0, slopes_k)
    own0, own1 = pl.pallas_call(
        own_kernel,
        in_specs=[IN_HBM, IN_HBM, IN_VMEM, IN_VMEM],
        out_shape=(shaped((half, columns), F32),) * 2,
        scratch_shapes=scratch(turned, turned) + semaphores(2),
        compiler_params=VMEM,
        cost_estimate=cost(2 * flops, 10**7),
    )(kept0, kept1, slopes_q, slopes_k)
    rows = half // 2

    def paired(first, dtype, other0, other1, *after):
        return pl.pallas_call(
            functools.partial(pair_kernel, first=first),
            in_specs=[IN_VMEM] * 6 + [IN_HBM] * len(after),
            out_shape=(shaped((rows, columns), dtype),) * 2,
            compiler_params=VMEM,
            cost_estimate=cost(flops, 6 * 10**6),
        )(own0, other0, partner_q, own1, other1, partner_k, *after)

    send0, send1 = paired(rows, BF16, late0, late1)
    keep0, keep1 = paired(0, F32, early0, early1, send1[:16, :128])
    for step in range(1, STEPS - 1):
        operands = (exchange(0, step, send0), keep0, exchange(1, step, send1), keep1)
        rows //= 2
        if step < STEPS - 2:
            pair = (shaped((rows, columns), F32), shaped((rows, columns), BF16))
            keep0, send0, keep1, send1 = pl.pallas_call(
                add_kernel, out_shape=pair + pair, compiler_params=VMEM
            )(*operands)
        else:
            keep, send = pl.pallas_call(
                join_kernel,
                out_shape=(shaped((rows, 2 * columns), F32), shaped((rows, 2 * columns), BF16)),
                compiler_params=VMEM,
            )(*operands)
    assert PARTNERS[0][STEPS - 1] == PARTNERS[1][STEPS - 1]
    received = exchange(0, STEPS - 1, send)
    qweight_grad, kweight_grad = pl.pallas_call(
        last_kernel, out_shape=(shaped((rows, columns), F32),) * 2, compiler_params=VMEM
    )(received, keep)
    value_grad = pl.pallas_call(
        values_kernel,
        out_shape=small,
        compiler_params=VMEM,
        cost_estimate=cost(10**9, 5 * 10**6),
    )(local_v, weighted_k, incoming)
    return qweight_grad, kweight_grad, value_grad


def solution(mesh):
    chips = mesh.devices.shape[0] // CORES
    split = Mesh(mesh.devices.reshape(chips, CORES, N_Y, N_Z), ("x",) + AXES)
    seq, cores = ("y", "z"), ("x", "core")
    both = P(seq, cores)
    return jax.shard_map(
        per_device,
        mesh=split,
        in_specs=(P(seq, None), both, both, both, both, both),
        out_specs=(both, both, both),
        check_vma=False,
    )
```

```python
import functools

import jax
import jax.numpy as jnp
import numpy as np
from jax import lax
from jax.experimental import pallas as pl
from jax.experimental.pallas import tpu as pltpu
from jax.sharding import Mesh, PartitionSpec as P

HEAD = 128
N_Y = 4
N_Z = 8
SEQ = N_Y * N_Z
CORES = 2
RANKS = CORES * SEQ
STEPS = 5
AXES = ("core", "y", "z")
MESSAGE = 40
BF16 = jnp.bfloat16
F32 = jnp.float32
VMEM = pltpu.CompilerParams(vmem_limit_bytes=20 * 2**20)
WIDE = pltpu.CompilerParams(vmem_limit_bytes=56 * 2**20)


def exchange_plan(stream, core):
    way = 1 - 2 * core
    if stream == 0:
        return [("z", way), ("y", way), ("z", -way), ("y", -way), ("z", 3 * way)]
    return [("y", way), ("z", way), ("y", -way), ("z", -way), ("z", 3 * way)]


def rank_of(core, y, z):
    return (core * N_Y + y) * N_Z + z


def partner_of(kind, core, y, z):
    axis, shift = kind
    if axis == "z":
        return rank_of(core, y, (z + shift * (1 - 2 * (z % 2))) % N_Z)
    return rank_of(core, (y + shift * (1 - 2 * (y % 2))) % N_Y, z)


def exchange_partners(stream):
    steps = []
    for step in range(STEPS):
        partners = {}
        for core in range(CORES):
            for y in range(N_Y):
                for z in range(N_Z):
                    partners[rank_of(core, y, z)] = partner_of(exchange_plan(stream, core)[step], core, y, z)
        steps.append(partners)
    return steps


def block_order(stream):
    steps = exchange_partners(stream)
    order = {rank: [rank % SEQ] for rank in range(RANKS)}
    for partners in reversed(steps):
        order = {rank: order[rank] + order[partners[rank]] for rank in range(RANKS)}
    for rank in range(RANKS):
        assert sorted(order[rank]) == list(range(SEQ))
    return np.array([order[rank] for rank in range(RANKS)], np.int32)


PARTNERS = [exchange_partners(stream) for stream in range(2)]
ORDERS = np.stack([block_order(stream) for stream in range(2)])


def dot(a, b, contract):
    return lax.dot_general(a, b, ((contract[:1], contract[1:]), ((), ())), preferred_element_type=F32)


def split3(value):
    high = value.astype(BF16)
    rest = value - high.astype(F32)
    middle = rest.astype(BF16)
    low = (rest - middle.astype(F32)).astype(BF16)
    return high, middle, low


def moves(sources, targets, semaphores, first=0):
    return [
        pltpu.make_async_copy(source, target, semaphores.at[first + at])
        for at, (source, target) in enumerate(zip(sources, targets))
    ]


def start_all(copies):
    for copy in copies:
        copy.start()


def prefix_sums(decay):
    heads, tokens = decay.shape
    rows = lax.broadcasted_iota(jnp.int32, (tokens, tokens), 0)
    columns = lax.broadcasted_iota(jnp.int32, (tokens, tokens), 1)
    lower = jnp.where(rows >= columns, 1.0, 0.0).astype(BF16)
    parts = jnp.concatenate([piece.astype(F32) for piece in split3(decay)], axis=0).astype(BF16)
    down = dot(lower, parts, (1, 1))
    across = dot(parts, lower, (1, 1))
    return (
        down[:, :heads] + down[:, heads : 2 * heads] + down[:, 2 * heads :],
        across[:heads] + across[heads : 2 * heads] + across[2 * heads :],
    )


def states_kernel(
    decay_hbm, query_hbm, key_hbm, value_hbm, grad_hbm, out_ref,
    decay_ref, query_ref, key_ref, value_ref, grad_ref, semaphores,
):
    heads, tokens = decay_ref.shape
    scaling = HEAD ** (-0.5)
    copies = moves(
        (decay_hbm, key_hbm, value_hbm, query_hbm, grad_hbm),
        (decay_ref, key_ref, value_ref, query_ref, grad_ref),
        semaphores,
    )
    start_all(copies)
    copies[0].wait()
    cumulative, _ = prefix_sums(decay_ref[...])
    total = cumulative[tokens - 1 :, :]
    from_start = jnp.exp(cumulative)
    to_end = jnp.exp(total - cumulative)
    per = SEQ // (2 * heads)
    span = HEAD // per
    line = lax.broadcasted_iota(jnp.int32, (MESSAGE - span, HEAD), 0)
    tails = []
    for head in range(heads):
        marks = split3(jnp.broadcast_to(total[:, head : head + 1], (MESSAGE - span, HEAD)))
        tail = jnp.where(
            line == 0, marks[0].astype(F32), jnp.where(line == 1, marks[1].astype(F32), marks[2].astype(F32))
        )
        tails.append(jnp.where(line < 3, tail, 0.0).astype(BF16))

    def emit(direction, head, state):
        state = state.astype(BF16)
        for piece in range(per):
            owner = (direction * heads + head) * per + piece
            out_ref[owner, :span, :] = state[piece * span : (piece + 1) * span, :]
            out_ref[owner, span:, :] = tails[head]

    copies[1].wait()
    copies[2].wait()
    for head in range(heads):
        part = slice(head * HEAD, (head + 1) * HEAD)
        x = key_ref[:, part].astype(F32)
        keys = (x * jax.nn.sigmoid(x)).astype(BF16)
        weighted = (keys.astype(F32) * to_end[:, head : head + 1]).astype(BF16)
        emit(0, head, dot(weighted, value_ref[:, part], (0, 0)))
    copies[3].wait()
    copies[4].wait()
    for head in range(heads):
        part = slice(head * HEAD, (head + 1) * HEAD)
        x = query_ref[:, part].astype(F32)
        queries = (x * jax.nn.sigmoid(x) * scaling).astype(BF16)
        weighted = (queries.astype(F32) * from_start[:, head : head + 1]).astype(BF16)
        emit(1, head, dot(weighted, grad_ref[:, part], (0, 0)))


def scan_kernel(place_ref, in_ref, out_ref):
    count = in_ref.shape[0]
    span = out_ref.shape[1]
    backward = place_ref[0] >= count // 2

    def step(at, carried):
        source = jnp.where(backward, count - 1 - at, at)
        out_ref[source] = carried.astype(BF16)
        message = in_ref[source].astype(F32)
        total = message[span : span + 1] + message[span + 1 : span + 2] + message[span + 2 : span + 3]
        return jnp.exp(total) * carried + message[:span]

    lax.fori_loop(0, count, step, jnp.zeros((span, HEAD), F32), unroll=4)


def local_kernel(
    decay_hbm, query_hbm, key_hbm, value_hbm, grad_hbm,
    gq_hbm, gk_hbm, gv_hbm, sq_hbm, sk_hbm, wo_hbm, wv_hbm, wk_hbm,
    decay_ref, query_ref, key_ref, value_ref, grad_ref,
    q_ref, k_ref, gq_ref, gk_ref, gv_ref, sq_ref, sk_ref, wo_ref, wv_ref, wk_ref, cum_ref, row_ref, semaphores,
):
    heads, tokens = decay_ref.shape
    scaling = HEAD ** (-0.5)
    copies = moves(
        (decay_hbm, query_hbm, key_hbm, value_hbm, grad_hbm),
        (decay_ref, query_ref, key_ref, value_ref, grad_ref),
        semaphores,
    )
    start_all(copies)
    writes = moves(
        (gq_ref, gk_ref, gv_ref, sq_ref, sk_ref, wo_ref, wv_ref, wk_ref),
        (gq_hbm, gk_hbm, gv_hbm, sq_hbm, sk_hbm, wo_hbm, wv_hbm, wk_hbm),
        semaphores,
        len(copies),
    )
    copies[0].wait()
    cum_ref[...], row_ref[...] = prefix_sums(decay_ref[...])
    for copy in copies[1:]:
        copy.wait()
    half = tokens // 2
    rows = lax.broadcasted_iota(jnp.int32, (half, half), 0)
    columns = lax.broadcasted_iota(jnp.int32, (half, half), 1)
    causal = rows >= columns
    for head in range(heads):
        part = slice(head * HEAD, (head + 1) * HEAD)
        line = slice(head, head + 1)
        x = query_ref[:, part].astype(F32)
        sigmoid = jax.nn.sigmoid(x)
        q_ref[:, part] = (x * sigmoid * scaling).astype(BF16)
        sq_ref[:, part] = (sigmoid * (1.0 + x * (1.0 - sigmoid)) * scaling).astype(BF16)
        x = key_ref[:, part].astype(F32)
        sigmoid = jax.nn.sigmoid(x)
        keys = (x * sigmoid).astype(BF16)
        k_ref[:, part] = keys
        sk_ref[:, part] = (sigmoid * (1.0 + x * (1.0 - sigmoid))).astype(BF16)
        cumulative = cum_ref[:, line]
        to_end = jnp.exp(cum_ref[tokens - 1 :, line] - cumulative)
        wo_ref[:, part] = (jnp.exp(cumulative) * grad_ref[:, part].astype(F32)).astype(BF16)
        wv_ref[:, part] = (to_end * value_ref[:, part].astype(F32)).astype(BF16)
        wk_ref[:, part] = (to_end * keys.astype(F32)).astype(BF16)

        def diagonal(block):
            spread = cum_ref[block, line] - row_ref[line, block]
            return jnp.where(causal, jnp.exp(jnp.minimum(spread, 0.0)), 0.0)

        early, late = slice(0, half), slice(half, tokens)
        border = cum_ref[half - 1 : half, line]
        decay_first = diagonal(early)
        decay_last = diagonal(late)
        decay_rows = jnp.exp(jnp.minimum(cum_ref[late, line] - border, 0.0))
        decay_columns = jnp.exp(jnp.minimum(border - row_ref[line, early], 0.0))

        def scores(left, right):
            first = (dot(left[early, part], right[early, part], (1, 1)) * decay_first).astype(BF16)
            across = (dot(left[late, part], right[early, part], (1, 1)) * decay_rows * decay_columns).astype(BF16)
            last = (dot(left[late, part], right[late, part], (1, 1)) * decay_last).astype(BF16)
            return first, across, last

        first, across, last = scores(grad_ref, value_ref)
        gq_ref[early, part] = dot(first, k_ref[early, part], (1, 0)).astype(BF16)
        gq_ref[late, part] = (dot(across, k_ref[early, part], (1, 0)) + dot(last, k_ref[late, part], (1, 0))).astype(BF16)
        gk_ref[early, part] = (dot(first, q_ref[early, part], (0, 0)) + dot(across, q_ref[late, part], (0, 0))).astype(BF16)
        gk_ref[late, part] = dot(last, q_ref[late, part], (0, 0)).astype(BF16)
        first, across, last = scores(q_ref, k_ref)
        gv_ref[early, part] = dot(first, grad_ref[early, part], (0, 0)) + dot(across, grad_ref[late, part], (0, 0))
        gv_ref[late, part] = dot(last, grad_ref[late, part], (0, 0))
    start_all(writes)
    for copy in writes:
        copy.wait()


def heads_kernel(
    states_hbm, wo_hbm, gq_hbm, sq_hbm, wv_hbm, gk_hbm, sk_hbm,
    slopes_q_ref, slopes_k_ref,
    states_ref, wo_ref, gq_ref, sq_ref, wv_ref, gk_ref, sk_ref, semaphores,
):
    heads = wo_ref.shape[1] // HEAD
    copies = moves(
        (wo_hbm, states_hbm, gq_hbm, sq_hbm, wv_hbm, gk_hbm, sk_hbm),
        (wo_ref, states_ref, gq_ref, sq_ref, wv_ref, gk_ref, sk_ref),
        semaphores,
    )
    start_all(copies)
    for stream, (weighted, local, slope, slopes) in enumerate(
        ((wo_ref, gq_ref, sq_ref, slopes_q_ref), (wv_ref, gk_ref, sk_ref, slopes_k_ref))
    ):
        for copy in copies[4 * stream : 4 * stream + 4 - stream]:
            copy.wait()
        for head in range(heads):
            part = slice(head * HEAD, (head + 1) * HEAD)
            state = slice((stream * heads + head) * HEAD, (stream * heads + head + 1) * HEAD)
            gradient = local[:, part].astype(F32) + dot(weighted[:, part], states_ref[state, :], (1, 1))
            slopes[:, part] = (gradient * slope[:, part].astype(F32)).astype(BF16)


def pair_kernel(own0_ref, rows0_ref, slopes0_ref, own1_ref, rows1_ref, slopes1_ref, *refs, first):
    out0_ref, out1_ref = refs[-2:]
    part = slice(first, first + out0_ref.shape[0])
    for own, rows, slopes, out in (
        (own0_ref, rows0_ref, slopes0_ref, out0_ref),
        (own1_ref, rows1_ref, slopes1_ref, out1_ref),
    ):
        out[...] = (own[part] + dot(rows[...], slopes[...], (1, 0))).astype(out.dtype)


def values_kernel(local_ref, weighted_ref, states_ref, out_ref):
    heads = out_ref.shape[1] // HEAD
    for head in range(heads):
        part = slice(head * HEAD, (head + 1) * HEAD)
        later = slice((heads + head) * HEAD, (heads + head + 1) * HEAD)
        out_ref[:, part] = (local_ref[:, part] + dot(weighted_ref[:, part], states_ref[later, :], (1, 0))).astype(BF16)


def arrange_kernel(
    place_ref, table_ref, input_hbm,
    late0_hbm, late1_hbm, early0_hbm, early1_hbm, kept0_hbm, kept1_hbm,
    input_ref, turned_ref, late0_ref, late1_ref, early0_ref, early1_ref, kept0_ref, kept1_ref, semaphores,
):
    tokens, width = input_ref.shape
    block = width // SEQ
    chunk = 384
    reads = moves(
        [input_hbm.at[:, at : at + chunk] for at in range(0, width, chunk)],
        [input_ref.at[:, at : at + chunk] for at in range(0, width, chunk)],
        semaphores,
    )
    start_all(reads)
    outs = (late0_ref, late1_ref, early0_ref, early1_ref, kept0_ref, kept1_ref)
    targets = (late0_hbm, late1_hbm, early0_hbm, early1_hbm, kept0_hbm, kept1_hbm)
    writes = moves(outs, targets, semaphores, len(reads))
    for at, copy in enumerate(reads):
        copy.wait()
        turned_ref[at * chunk : (at + 1) * chunk, :] = input_ref[:, at * chunk : (at + 1) * chunk].T
    firsts = (3 * SEQ // 4, 3 * SEQ // 4, SEQ // 2, SEQ // 2, 0, 0)
    for out, write, stream, first in zip(outs, writes, (0, 1) * 3, firsts):
        for at in range(out.shape[0] // block):
            entry = (stream * RANKS + place_ref[0]) * SEQ + first + at
            start = pl.multiple_of(table_ref[entry] * block, block)
            out[at * block : (at + 1) * block, :] = turned_ref[pl.ds(start, block), :]
        write.start()
    for copy in writes:
        copy.wait()


def own_kernel(
    rows0_hbm, rows1_hbm, slopes0_ref, slopes1_ref, out0_ref, out1_ref, rows0_ref, rows1_ref, semaphores
):
    copies = moves((rows0_hbm, rows1_hbm), (rows0_ref, rows1_ref), semaphores)
    start_all(copies)
    for copy, rows, slopes, out in zip(
        copies, (rows0_ref, rows1_ref), (slopes0_ref, slopes1_ref), (out0_ref, out1_ref)
    ):
        copy.wait()
        out[...] = dot(rows[...], slopes[...], (1, 0))


def add_kernel(received_ref, kept_ref, keep_ref, send_ref):
    half = keep_ref.shape[0]
    keep_ref[...] = kept_ref[:half] + received_ref[:half].astype(F32)
    send_ref[...] = (kept_ref[half:] + received_ref[half:].astype(F32)).astype(BF16)


def join_kernel(received0_ref, kept0_ref, received1_ref, kept1_ref, keep_ref, send_ref):
    half, columns = keep_ref.shape[0], kept0_ref.shape[1]
    for stream, (received, kept) in enumerate(((received0_ref, kept0_ref), (received1_ref, kept1_ref))):
        part = slice(stream * columns, (stream + 1) * columns)
        keep_ref[:, part] = kept[:half] + received[:half].astype(F32)
        send_ref[:, part] = (kept[half:] + received[half:].astype(F32)).astype(BF16)


def last_kernel(received_ref, kept_ref, out0_ref, out1_ref):
    columns = out0_ref.shape[1]
    for stream, out in enumerate((out0_ref, out1_ref)):
        part = slice(stream * columns, (stream + 1) * columns)
        out[...] = kept_ref[:, part] + received_ref[:, part].astype(F32)


def shaped(shape, dtype):
    return jax.ShapeDtypeStruct(shape, dtype)


def cost(flops, moved):
    return pl.CostEstimate(flops=flops, bytes_accessed=moved, transcendentals=0)


IN_HBM = pl.BlockSpec(memory_space=pltpu.HBM)
IN_VMEM = pl.BlockSpec(memory_space=pltpu.VMEM)


def per_device(layer_input, query_preact, key_preact, value_rows, output_grad, log_decay):
    tokens, heads = log_decay.shape
    columns = query_preact.shape[1]
    width = layer_input.shape[1]
    core, y, z = (lax.axis_index(axis) for axis in AXES)
    place = y * N_Z + z
    half = width // 2
    small, large = shaped((tokens, columns), BF16), shaped((tokens, columns), F32)
    partial = shaped((half, columns), BF16)
    turned = shaped((half, tokens), BF16)
    decay = shaped((heads, tokens), F32)
    states_shape = shaped((2 * heads * HEAD, HEAD), BF16)
    arguments = (log_decay.T, query_preact, key_preact, value_rows, output_grad)

    def scratch(*shapes):
        return [pltpu.VMEM(one.shape, one.dtype) for one in shapes]

    def semaphores(count):
        return [pltpu.SemaphoreType.DMA((count,))]

    states = pl.pallas_call(
        states_kernel,
        in_specs=[IN_HBM] * 5,
        out_shape=shaped((SEQ, MESSAGE, HEAD), BF16),
        scratch_shapes=scratch(decay, small, small, small, small) + semaphores(5),
        compiler_params=WIDE,
        cost_estimate=cost(10**9, 4 * 10**6),
    )(*arguments)
    states = lax.all_to_all(states, ("y", "z"), 0, 0, tiled=True)
    local_shapes = (small, small, large, small, small, small, small, small)
    local_q, local_k, local_v, slope_q, slope_k, weighted_o, weighted_v, weighted_k = pl.pallas_call(
        local_kernel,
        in_specs=[IN_HBM] * 5,
        out_specs=(IN_HBM,) * 8,
        out_shape=local_shapes,
        scratch_shapes=scratch(decay, *(small,) * 6, *local_shapes, shaped((tokens, heads), F32), decay)
        + semaphores(13),
        compiler_params=WIDE,
        cost_estimate=cost(6 * 10**10, 10**7),
    )(*arguments)
    rank = (core * SEQ + place)[None].astype(jnp.int32)
    table = jnp.asarray(ORDERS.reshape(-1))
    chunks = width // 384

    quarter = shaped((half // 2, tokens), BF16)
    arranged = (quarter,) * 4 + (turned,) * 2
    late0, late1, early0, early1, kept0, kept1 = pl.pallas_call(
        arrange_kernel,
        in_specs=[pl.BlockSpec(memory_space=pltpu.SMEM)] * 2 + [IN_HBM],
        out_specs=(IN_HBM,) * 6,
        out_shape=arranged,
        scratch_shapes=scratch(shaped((tokens, width), BF16), shaped((width, tokens), BF16), *arranged)
        + semaphores(chunks + 6),
        compiler_params=WIDE,
        cost_estimate=cost(10**9, 10**7),
    )(rank, table, layer_input)
    states, kept0 = lax.optimization_barrier((states, kept0))
    span = 2 * heads * HEAD // SEQ
    incoming = pl.pallas_call(
        scan_kernel,
        in_specs=[pl.BlockSpec(memory_space=pltpu.SMEM), IN_VMEM],
        out_shape=shaped((SEQ, span, HEAD), BF16),
        compiler_params=VMEM,
    )(place[None].astype(jnp.int32), states)
    incoming, early0, early1 = lax.optimization_barrier((incoming, early0, early1))
    incoming = lax.all_to_all(incoming, ("y", "z"), 0, 0, tiled=True).reshape(2 * heads * HEAD, HEAD)
    flops = 2 * half * columns * tokens

    def exchange(stream, step, array):
        return lax.ppermute(array, AXES, sorted(PARTNERS[stream][step].items()))

    late0, late1 = exchange(0, 0, late0), exchange(1, 0, late1)
    early0, early1 = exchange(0, 0, early0), exchange(1, 0, early1)
    early0, early1, kept0 = lax.optimization_barrier((early0, early1, kept0))
    slopes_q, slopes_k = pl.pallas_call(
        heads_kernel,
        in_specs=[pl.BlockSpec(memory_space=pl.ANY)] + [IN_HBM] * 6,
        out_shape=(small, small),
        scratch_shapes=scratch(states_shape, *(small,) * 6) + semaphores(7),
        compiler_params=WIDE,
        cost_estimate=cost(10**9, 4 * 10**6),
    )(incoming, weighted_o, local_q, slope_q, weighted_v, local_k, slope_k)
    partner_q, partner_k = exchange(0, 0, slopes_q), exchange(1, 0, slopes_k)
    own0, own1 = pl.pallas_call(
        own_kernel,
        in_specs=[IN_HBM, IN_HBM, IN_VMEM, IN_VMEM],
        out_shape=(shaped((half, columns), F32),) * 2,
        scratch_shapes=scratch(turned, turned) + semaphores(2),
        compiler_params=VMEM,
        cost_estimate=cost(2 * flops, 10**7),
    )(kept0, kept1, slopes_q, slopes_k)
    rows = half // 2

    def paired(first, dtype, other0, other1, *after):
        return pl.pallas_call(
            functools.partial(pair_kernel, first=first),
            in_specs=[IN_VMEM] * 6 + [IN_HBM] * len(after),
            out_shape=(shaped((rows, columns), dtype),) * 2,
            compiler_params=VMEM,
            cost_estimate=cost(flops, 6 * 10**6),
        )(own0, other0, partner_q, own1, other1, partner_k, *after)

    send0, send1 = paired(rows, BF16, late0, late1)
    keep0, keep1 = paired(0, F32, early0, early1, send1[:16, :128])
    keeps, sends = [keep0, keep1], [send0, send1]
    for step in range(1, STEPS - 1):
        received = [exchange(stream, step, sends[stream]) for stream in range(2)]
        rows //= 2
        if step < STEPS - 2:
            pairs = [
                pl.pallas_call(
                    add_kernel,
                    out_shape=(shaped((rows, columns), F32), shaped((rows, columns), BF16)),
                    compiler_params=VMEM,
                )(received[stream], keeps[stream])
                for stream in range(2)
            ]
            keeps, sends = [one[0] for one in pairs], [one[1] for one in pairs]
        else:
            keep, send = pl.pallas_call(
                join_kernel,
                out_shape=(shaped((rows, 2 * columns), F32), shaped((rows, 2 * columns), BF16)),
                compiler_params=VMEM,
            )(received[0], keeps[0], received[1], keeps[1])
    assert PARTNERS[0][STEPS - 1] == PARTNERS[1][STEPS - 1]
    received = exchange(0, STEPS - 1, send)
    qweight_grad, kweight_grad = pl.pallas_call(
        last_kernel, out_shape=(shaped((rows, columns), F32),) * 2, compiler_params=VMEM
    )(received, keep)
    value_grad = pl.pallas_call(
        values_kernel,
        out_shape=small,
        compiler_params=VMEM,
        cost_estimate=cost(10**9, 5 * 10**6),
    )(local_v, weighted_k, incoming)
    return qweight_grad, kweight_grad, value_grad


def solution(mesh):
    chips = mesh.devices.shape[0] // CORES
    split = Mesh(mesh.devices.reshape(chips, CORES, N_Y, N_Z), ("x",) + AXES)
    seq, cores = ("y", "z"), ("x", "core")
    both = P(seq, cores)
    return jax.shard_map(
        per_device,
        mesh=split,
        in_specs=(P(seq, None), both, both, both, both, both),
        out_specs=(both, both, both),
        check_vma=False,
    )
```

```python
import functools

import jax
import jax.numpy as jnp
import numpy as np
from jax import lax
from jax.experimental import pallas as pl
from jax.experimental.pallas import tpu as pltpu
from jax.sharding import Mesh, PartitionSpec as P

HEAD = 128
N_Y = 4
N_Z = 8
SEQ = N_Y * N_Z
CORES = 2
RANKS = CORES * SEQ
STEPS = 5
AXES = ("core", "y", "z")
MESSAGE = 40
BF16 = jnp.bfloat16
F32 = jnp.float32
VMEM = pltpu.CompilerParams(vmem_limit_bytes=20 * 2**20)
WIDE = pltpu.CompilerParams(vmem_limit_bytes=56 * 2**20)


def exchange_plan(stream, core):
    way = 1 - 2 * core
    if stream == 0:
        return [("z", way), ("y", way), ("z", -way), ("y", -way), ("z", 3 * way)]
    return [("y", way), ("z", way), ("y", -way), ("z", -way), ("z", 3 * way)]


def rank_of(core, y, z):
    return (core * N_Y + y) * N_Z + z


def partner_of(kind, core, y, z):
    axis, shift = kind
    if axis == "z":
        return rank_of(core, y, (z + shift * (1 - 2 * (z % 2))) % N_Z)
    return rank_of(core, (y + shift * (1 - 2 * (y % 2))) % N_Y, z)


def exchange_partners(stream):
    steps = []
    for step in range(STEPS):
        partners = {}
        for core in range(CORES):
            for y in range(N_Y):
                for z in range(N_Z):
                    partners[rank_of(core, y, z)] = partner_of(exchange_plan(stream, core)[step], core, y, z)
        steps.append(partners)
    return steps


def block_order(stream):
    steps = exchange_partners(stream)
    order = {rank: [rank % SEQ] for rank in range(RANKS)}
    for partners in reversed(steps):
        order = {rank: order[rank] + order[partners[rank]] for rank in range(RANKS)}
    for rank in range(RANKS):
        assert sorted(order[rank]) == list(range(SEQ))
    return np.array([order[rank] for rank in range(RANKS)], np.int32)


PARTNERS = [exchange_partners(stream) for stream in range(2)]
ORDERS = np.stack([block_order(stream) for stream in range(2)])


def dot(a, b, contract):
    return lax.dot_general(a, b, ((contract[:1], contract[1:]), ((), ())), preferred_element_type=F32)


def split3(value):
    high = value.astype(BF16)
    rest = value - high.astype(F32)
    middle = rest.astype(BF16)
    low = (rest - middle.astype(F32)).astype(BF16)
    return high, middle, low


def moves(sources, targets, semaphores, first=0):
    return [
        pltpu.make_async_copy(source, target, semaphores.at[first + at])
        for at, (source, target) in enumerate(zip(sources, targets))
    ]


def start_all(copies):
    for copy in copies:
        copy.start()


def prefix_sums(decay):
    heads, tokens = decay.shape
    rows = lax.broadcasted_iota(jnp.int32, (tokens, tokens), 0)
    columns = lax.broadcasted_iota(jnp.int32, (tokens, tokens), 1)
    lower = jnp.where(rows >= columns, 1.0, 0.0).astype(BF16)
    parts = jnp.concatenate([piece.astype(F32) for piece in split3(decay)], axis=0).astype(BF16)
    down = dot(lower, parts, (1, 1))
    across = dot(parts, lower, (1, 1))
    return (
        down[:, :heads] + down[:, heads : 2 * heads] + down[:, 2 * heads :],
        across[:heads] + across[heads : 2 * heads] + across[2 * heads :],
    )


def states_kernel(
    decay_hbm, query_hbm, key_hbm, value_hbm, grad_hbm, out_ref,
    decay_ref, query_ref, key_ref, value_ref, grad_ref, semaphores,
):
    heads, tokens = decay_ref.shape
    scaling = HEAD ** (-0.5)
    copies = moves(
        (decay_hbm, key_hbm, value_hbm, query_hbm, grad_hbm),
        (decay_ref, key_ref, value_ref, query_ref, grad_ref),
        semaphores,
    )
    start_all(copies)
    copies[0].wait()
    cumulative, _ = prefix_sums(decay_ref[...])
    total = cumulative[tokens - 1 :, :]
    from_start = jnp.exp(cumulative)
    to_end = jnp.exp(total - cumulative)
    per = SEQ // (2 * heads)
    span = HEAD // per
    line = lax.broadcasted_iota(jnp.int32, (MESSAGE - span, HEAD), 0)
    tails = []
    for head in range(heads):
        marks = split3(jnp.broadcast_to(total[:, head : head + 1], (MESSAGE - span, HEAD)))
        tail = jnp.where(
            line == 0, marks[0].astype(F32), jnp.where(line == 1, marks[1].astype(F32), marks[2].astype(F32))
        )
        tails.append(jnp.where(line < 3, tail, 0.0).astype(BF16))

    def emit(direction, head, state):
        state = state.astype(BF16)
        for piece in range(per):
            owner = (direction * heads + head) * per + piece
            out_ref[owner, :span, :] = state[piece * span : (piece + 1) * span, :]
            out_ref[owner, span:, :] = tails[head]

    copies[1].wait()
    copies[2].wait()
    for head in range(heads):
        part = slice(head * HEAD, (head + 1) * HEAD)
        x = key_ref[:, part].astype(F32)
        keys = (x * jax.nn.sigmoid(x)).astype(BF16)
        weighted = (keys.astype(F32) * to_end[:, head : head + 1]).astype(BF16)
        emit(0, head, dot(weighted, value_ref[:, part], (0, 0)))
    copies[3].wait()
    copies[4].wait()
    for head in range(heads):
        part = slice(head * HEAD, (head + 1) * HEAD)
        x = query_ref[:, part].astype(F32)
        queries = (x * jax.nn.sigmoid(x) * scaling).astype(BF16)
        weighted = (queries.astype(F32) * from_start[:, head : head + 1]).astype(BF16)
        emit(1, head, dot(weighted, grad_ref[:, part], (0, 0)))


def scan_kernel(place_ref, in_ref, out_ref):
    count = in_ref.shape[0]
    span = out_ref.shape[1]
    backward = place_ref[0] >= count // 2

    def step(at, carried):
        source = jnp.where(backward, count - 1 - at, at)
        out_ref[source] = carried.astype(BF16)
        message = in_ref[source].astype(F32)
        total = message[span : span + 1] + message[span + 1 : span + 2] + message[span + 2 : span + 3]
        return jnp.exp(total) * carried + message[:span]

    lax.fori_loop(0, count, step, jnp.zeros((span, HEAD), F32), unroll=4)


def local_kernel(
    decay_hbm, query_hbm, key_hbm, value_hbm, grad_hbm,
    gq_hbm, gk_hbm, gv_hbm, sq_hbm, sk_hbm, wo_hbm, wv_hbm, wk_hbm,
    decay_ref, query_ref, key_ref, value_ref, grad_ref,
    q_ref, k_ref, gq_ref, gk_ref, gv_ref, sq_ref, sk_ref, wo_ref, wv_ref, wk_ref, cum_ref, row_ref, semaphores,
):
    heads, tokens = decay_ref.shape
    scaling = HEAD ** (-0.5)
    copies = moves(
        (decay_hbm, query_hbm, key_hbm, value_hbm, grad_hbm),
        (decay_ref, query_ref, key_ref, value_ref, grad_ref),
        semaphores,
    )
    start_all(copies)
    writes = moves(
        (gq_ref, gk_ref, gv_ref, sq_ref, sk_ref, wo_ref, wv_ref, wk_ref),
        (gq_hbm, gk_hbm, gv_hbm, sq_hbm, sk_hbm, wo_hbm, wv_hbm, wk_hbm),
        semaphores,
        len(copies),
    )
    copies[0].wait()
    cum_ref[...], row_ref[...] = prefix_sums(decay_ref[...])
    for copy in copies[1:]:
        copy.wait()
    half = tokens // 2
    rows = lax.broadcasted_iota(jnp.int32, (half, half), 0)
    columns = lax.broadcasted_iota(jnp.int32, (half, half), 1)
    causal = rows >= columns
    for head in range(heads):
        part = slice(head * HEAD, (head + 1) * HEAD)
        line = slice(head, head + 1)
        x = query_ref[:, part].astype(F32)
        sigmoid = jax.nn.sigmoid(x)
        q_ref[:, part] = (x * sigmoid * scaling).astype(BF16)
        sq_ref[:, part] = (sigmoid * (1.0 + x * (1.0 - sigmoid)) * scaling).astype(BF16)
        x = key_ref[:, part].astype(F32)
        sigmoid = jax.nn.sigmoid(x)
        keys = (x * sigmoid).astype(BF16)
        k_ref[:, part] = keys
        sk_ref[:, part] = (sigmoid * (1.0 + x * (1.0 - sigmoid))).astype(BF16)
        cumulative = cum_ref[:, line]
        to_end = jnp.exp(cum_ref[tokens - 1 :, line] - cumulative)
        wo_ref[:, part] = (jnp.exp(cumulative) * grad_ref[:, part].astype(F32)).astype(BF16)
        wv_ref[:, part] = (to_end * value_ref[:, part].astype(F32)).astype(BF16)
        wk_ref[:, part] = (to_end * keys.astype(F32)).astype(BF16)

        def diagonal(block):
            spread = cum_ref[block, line] - row_ref[line, block]
            return jnp.where(causal, jnp.exp(jnp.minimum(spread, 0.0)), 0.0)

        early, late = slice(0, half), slice(half, tokens)
        border = cum_ref[half - 1 : half, line]
        decay_first = diagonal(early)
        decay_last = diagonal(late)
        decay_rows = jnp.exp(jnp.minimum(cum_ref[late, line] - border, 0.0))
        decay_columns = jnp.exp(jnp.minimum(border - row_ref[line, early], 0.0))

        def scores(left, right):
            first = (dot(left[early, part], right[early, part], (1, 1)) * decay_first).astype(BF16)
            across = (dot(left[late, part], right[early, part], (1, 1)) * decay_rows * decay_columns).astype(BF16)
            last = (dot(left[late, part], right[late, part], (1, 1)) * decay_last).astype(BF16)
            return first, across, last

        first, across, last = scores(grad_ref, value_ref)
        gq_ref[early, part] = dot(first, k_ref[early, part], (1, 0)).astype(BF16)
        gq_ref[late, part] = (dot(across, k_ref[early, part], (1, 0)) + dot(last, k_ref[late, part], (1, 0))).astype(BF16)
        gk_ref[early, part] = (dot(first, q_ref[early, part], (0, 0)) + dot(across, q_ref[late, part], (0, 0))).astype(BF16)
        gk_ref[late, part] = dot(last, q_ref[late, part], (0, 0)).astype(BF16)
        first, across, last = scores(q_ref, k_ref)
        gv_ref[early, part] = dot(first, grad_ref[early, part], (0, 0)) + dot(across, grad_ref[late, part], (0, 0))
        gv_ref[late, part] = dot(last, grad_ref[late, part], (0, 0))
    start_all(writes)
    for copy in writes:
        copy.wait()


def heads_kernel(
    states_hbm, wo_hbm, gq_hbm, sq_hbm, wv_hbm, gk_hbm, sk_hbm,
    slopes_q_ref, slopes_k_ref,
    states_ref, wo_ref, gq_ref, sq_ref, wv_ref, gk_ref, sk_ref, semaphores,
):
    heads = wo_ref.shape[1] // HEAD
    copies = moves(
        (wo_hbm, states_hbm, gq_hbm, sq_hbm, wv_hbm, gk_hbm, sk_hbm),
        (wo_ref, states_ref, gq_ref, sq_ref, wv_ref, gk_ref, sk_ref),
        semaphores,
    )
    start_all(copies)
    for stream, (weighted, local, slope, slopes) in enumerate(
        ((wo_ref, gq_ref, sq_ref, slopes_q_ref), (wv_ref, gk_ref, sk_ref, slopes_k_ref))
    ):
        for copy in copies[4 * stream : 4 * stream + 4 - stream]:
            copy.wait()
        for head in range(heads):
            part = slice(head * HEAD, (head + 1) * HEAD)
            state = slice((stream * heads + head) * HEAD, (stream * heads + head + 1) * HEAD)
            gradient = local[:, part].astype(F32) + dot(weighted[:, part], states_ref[state, :], (1, 1))
            slopes[:, part] = (gradient * slope[:, part].astype(F32)).astype(BF16)


def pair_kernel(own_ref, rows_ref, slopes_ref, *refs, first):
    out_ref = refs[-1]
    part = slice(first, first + out_ref.shape[0])
    out_ref[...] = (own_ref[part] + dot(rows_ref[...], slopes_ref[...], (1, 0))).astype(out_ref.dtype)


def values_kernel(local_ref, weighted_ref, states_ref, out_ref):
    heads = out_ref.shape[1] // HEAD
    for head in range(heads):
        part = slice(head * HEAD, (head + 1) * HEAD)
        later = slice((heads + head) * HEAD, (heads + head + 1) * HEAD)
        out_ref[:, part] = (local_ref[:, part] + dot(weighted_ref[:, part], states_ref[later, :], (1, 0))).astype(BF16)


def arrange_kernel(
    place_ref, table_ref, input_hbm,
    late0_hbm, late1_hbm, early0_hbm, early1_hbm, kept0_hbm, kept1_hbm,
    input_ref, turned_ref, late0_ref, late1_ref, early0_ref, early1_ref, kept0_ref, kept1_ref, semaphores,
):
    tokens, width = input_ref.shape
    block = width // SEQ
    chunk = 384
    reads = moves(
        [input_hbm.at[:, at : at + chunk] for at in range(0, width, chunk)],
        [input_ref.at[:, at : at + chunk] for at in range(0, width, chunk)],
        semaphores,
    )
    start_all(reads)
    outs = (late0_ref, late1_ref, early0_ref, early1_ref, kept0_ref, kept1_ref)
    targets = (late0_hbm, late1_hbm, early0_hbm, early1_hbm, kept0_hbm, kept1_hbm)
    writes = moves(outs, targets, semaphores, len(reads))
    for at, copy in enumerate(reads):
        copy.wait()
        turned_ref[at * chunk : (at + 1) * chunk, :] = input_ref[:, at * chunk : (at + 1) * chunk].T
    firsts = (3 * SEQ // 4, 3 * SEQ // 4, SEQ // 2, SEQ // 2, 0, 0)
    for out, write, stream, first in zip(outs, writes, (0, 1) * 3, firsts):
        for at in range(out.shape[0] // block):
            entry = (stream * RANKS + place_ref[0]) * SEQ + first + at
            start = pl.multiple_of(table_ref[entry] * block, block)
            out[at * block : (at + 1) * block, :] = turned_ref[pl.ds(start, block), :]
        write.start()
    for copy in writes:
        copy.wait()


def own_kernel(
    rows0_hbm, rows1_hbm, slopes0_ref, slopes1_ref, out0_ref, out1_ref, rows0_ref, rows1_ref, semaphores
):
    copies = moves((rows0_hbm, rows1_hbm), (rows0_ref, rows1_ref), semaphores)
    start_all(copies)
    for copy, rows, slopes, out in zip(
        copies, (rows0_ref, rows1_ref), (slopes0_ref, slopes1_ref), (out0_ref, out1_ref)
    ):
        copy.wait()
        out[...] = dot(rows[...], slopes[...], (1, 0))


def add_kernel(received_ref, kept_ref, keep_ref, send_ref):
    half = keep_ref.shape[0]
    keep_ref[...] = kept_ref[:half] + received_ref[:half].astype(F32)
    send_ref[...] = (kept_ref[half:] + received_ref[half:].astype(F32)).astype(BF16)


def last_one_kernel(received_ref, kept_ref, mark_ref, out_ref):
    out_ref[...] = kept_ref[...] + received_ref[...].astype(F32)


def shaped(shape, dtype):
    return jax.ShapeDtypeStruct(shape, dtype)


def cost(flops, moved):
    return pl.CostEstimate(flops=flops, bytes_accessed=moved, transcendentals=0)


IN_HBM = pl.BlockSpec(memory_space=pltpu.HBM)
IN_VMEM = pl.BlockSpec(memory_space=pltpu.VMEM)


def per_device(layer_input, query_preact, key_preact, value_rows, output_grad, log_decay):
    tokens, heads = log_decay.shape
    columns = query_preact.shape[1]
    width = layer_input.shape[1]
    core, y, z = (lax.axis_index(axis) for axis in AXES)
    place = y * N_Z + z
    half = width // 2
    small, large = shaped((tokens, columns), BF16), shaped((tokens, columns), F32)
    partial = shaped((half, columns), BF16)
    turned = shaped((half, tokens), BF16)
    decay = shaped((heads, tokens), F32)
    states_shape = shaped((2 * heads * HEAD, HEAD), BF16)
    arguments = (log_decay.T, query_preact, key_preact, value_rows, output_grad)

    def scratch(*shapes):
        return [pltpu.VMEM(one.shape, one.dtype) for one in shapes]

    def semaphores(count):
        return [pltpu.SemaphoreType.DMA((count,))]

    states = pl.pallas_call(
        states_kernel,
        in_specs=[IN_HBM] * 5,
        out_shape=shaped((SEQ, MESSAGE, HEAD), BF16),
        scratch_shapes=scratch(decay, small, small, small, small) + semaphores(5),
        compiler_params=WIDE,
        cost_estimate=cost(10**9, 4 * 10**6),
    )(*arguments)
    states = lax.all_to_all(states, ("y", "z"), 0, 0, tiled=True)
    local_shapes = (small, small, large, small, small, small, small, small)
    local_q, local_k, local_v, slope_q, slope_k, weighted_o, weighted_v, weighted_k = pl.pallas_call(
        local_kernel,
        in_specs=[IN_HBM] * 5,
        out_specs=(IN_HBM,) * 8,
        out_shape=local_shapes,
        scratch_shapes=scratch(decay, *(small,) * 6, *local_shapes, shaped((tokens, heads), F32), decay)
        + semaphores(13),
        compiler_params=WIDE,
        cost_estimate=cost(6 * 10**10, 10**7),
    )(*arguments)
    rank = (core * SEQ + place)[None].astype(jnp.int32)
    table = jnp.asarray(ORDERS.reshape(-1))
    chunks = width // 384

    quarter = shaped((half // 2, tokens), BF16)
    arranged = (quarter,) * 4 + (turned,) * 2
    late0, late1, early0, early1, kept0, kept1 = pl.pallas_call(
        arrange_kernel,
        in_specs=[pl.BlockSpec(memory_space=pltpu.SMEM)] * 2 + [IN_HBM],
        out_specs=(IN_HBM,) * 6,
        out_shape=arranged,
        scratch_shapes=scratch(shaped((tokens, width), BF16), shaped((width, tokens), BF16), *arranged)
        + semaphores(chunks + 6),
        compiler_params=WIDE,
        cost_estimate=cost(10**9, 10**7),
    )(rank, table, layer_input)
    states, kept0 = lax.optimization_barrier((states, kept0))
    span = 2 * heads * HEAD // SEQ
    incoming = pl.pallas_call(
        scan_kernel,
        in_specs=[pl.BlockSpec(memory_space=pltpu.SMEM), IN_VMEM],
        out_shape=shaped((SEQ, span, HEAD), BF16),
        compiler_params=VMEM,
    )(place[None].astype(jnp.int32), states)
    incoming, early0, early1 = lax.optimization_barrier((incoming, early0, early1))
    incoming = lax.all_to_all(incoming, ("y", "z"), 0, 0, tiled=True).reshape(2 * heads * HEAD, HEAD)
    flops = 2 * half * columns * tokens

    def exchange(stream, step, array):
        return lax.ppermute(array, AXES, sorted(PARTNERS[stream][step].items()))

    late0, late1 = exchange(0, 0, late0), exchange(1, 0, late1)
    early0, early1 = exchange(0, 0, early0), exchange(1, 0, early1)
    early0, early1, kept0 = lax.optimization_barrier((early0, early1, kept0))
    slopes_q, slopes_k = pl.pallas_call(
        heads_kernel,
        in_specs=[pl.BlockSpec(memory_space=pl.ANY)] + [IN_HBM] * 6,
        out_shape=(small, small),
        scratch_shapes=scratch(states_shape, *(small,) * 6) + semaphores(7),
        compiler_params=WIDE,
        cost_estimate=cost(10**9, 4 * 10**6),
    )(incoming, weighted_o, local_q, slope_q, weighted_v, local_k, slope_k)
    partner_q, partner_k = exchange(0, 0, slopes_q), exchange(1, 0, slopes_k)
    own0, own1 = pl.pallas_call(
        own_kernel,
        in_specs=[IN_HBM, IN_HBM, IN_VMEM, IN_VMEM],
        out_shape=(shaped((half, columns), F32),) * 2,
        scratch_shapes=scratch(turned, turned) + semaphores(2),
        compiler_params=VMEM,
        cost_estimate=cost(2 * flops, 10**7),
    )(kept0, kept1, slopes_q, slopes_k)
    rows = half // 2

    def paired(first, dtype, *operands):
        return pl.pallas_call(
            functools.partial(pair_kernel, first=first),
            in_specs=[IN_VMEM] * 3 + [IN_HBM] * (len(operands) - 3),
            out_shape=shaped((rows, columns), dtype),
            compiler_params=VMEM,
            cost_estimate=cost(flops // 2, 3 * 10**6),
        )(*operands)

    send0 = paired(rows, BF16, own0, late0, partner_q)
    send1 = paired(rows, BF16, own1, late1, partner_k)
    after = send1[:16, :128]
    keep0 = paired(0, F32, own0, early0, partner_q, after)
    keep1 = paired(0, F32, own1, early1, partner_k, after)
    keeps, sends = [keep0, keep1], [send0, send1]
    for step in range(1, STEPS - 1):
        received = [exchange(stream, step, sends[stream]) for stream in range(2)]
        rows //= 2
        if step < STEPS - 2:
            pairs = [
                pl.pallas_call(
                    add_kernel,
                    out_shape=(shaped((rows, columns), F32), shaped((rows, columns), BF16)),
                    compiler_params=VMEM,
                )(received[stream], keeps[stream])
                for stream in range(2)
            ]
            keeps, sends = [one[0] for one in pairs], [one[1] for one in pairs]
        else:
            pairs = [
                pl.pallas_call(
                    add_kernel,
                    out_shape=(shaped((rows, columns), F32), shaped((rows, columns), BF16)),
                    compiler_params=VMEM,
                )(received[stream], keeps[stream])
                for stream in range(2)
            ]
            keeps, sends = [one[0] for one in pairs], [one[1] for one in pairs]
    other_core = [(rank, (rank + SEQ) % RANKS) for rank in range(RANKS)]
    mark = lax.ppermute(sends[1][:16, :128], AXES, other_core)
    gated, mark = lax.optimization_barrier((sends[0], mark))
    sends = (gated, sends[1], mark)
    qweight_grad, kweight_grad = [
        pl.pallas_call(
            last_one_kernel,
            in_specs=[IN_VMEM, IN_VMEM, pl.BlockSpec(memory_space=pl.ANY)],
            out_shape=shaped((rows, columns), F32),
            compiler_params=VMEM,
        )(exchange(stream, STEPS - 1, sends[stream]), keeps[stream], sends[2])
        for stream in range(2)
    ]
    value_grad = pl.pallas_call(
        values_kernel,
        out_shape=small,
        compiler_params=VMEM,
        cost_estimate=cost(10**9, 5 * 10**6),
    )(local_v, weighted_k, incoming)
    return qweight_grad, kweight_grad, value_grad


def solution(mesh):
    chips = mesh.devices.shape[0] // CORES
    split = Mesh(mesh.devices.reshape(chips, CORES, N_Y, N_Z), ("x",) + AXES)
    seq, cores = ("y", "z"), ("x", "core")
    both = P(seq, cores)
    return jax.shard_map(
        per_device,
        mesh=split,
        in_specs=(P(seq, None), both, both, both, both, both),
        out_specs=(both, both, both),
        check_vma=False,
    )
```

```python
import functools

import jax
import jax.numpy as jnp
import numpy as np
from jax import lax
from jax.experimental import pallas as pl
from jax.experimental.pallas import tpu as pltpu
from jax.sharding import Mesh, PartitionSpec as P

HEAD = 128
N_Y = 4
N_Z = 8
SEQ = N_Y * N_Z
CORES = 2
RANKS = CORES * SEQ
STEPS = 5
AXES = ("core", "y", "z")
MESSAGE = 40
BF16 = jnp.bfloat16
F32 = jnp.float32
VMEM = pltpu.CompilerParams(vmem_limit_bytes=20 * 2**20)
WIDE = pltpu.CompilerParams(vmem_limit_bytes=56 * 2**20)


def exchange_plan(stream, core):
    way = 1 - 2 * core
    if stream == 0:
        return [("z", way), ("y", way), ("z", -way), ("y", -way), ("z", 3 * way)]
    return [("y", way), ("z", way), ("y", -way), ("z", -way), ("z", 3 * way)]


def rank_of(core, y, z):
    return (core * N_Y + y) * N_Z + z


def partner_of(kind, core, y, z):
    axis, shift = kind
    if axis == "z":
        return rank_of(core, y, (z + shift * (1 - 2 * (z % 2))) % N_Z)
    return rank_of(core, (y + shift * (1 - 2 * (y % 2))) % N_Y, z)


def exchange_partners(stream):
    steps = []
    for step in range(STEPS):
        partners = {}
        for core in range(CORES):
            for y in range(N_Y):
                for z in range(N_Z):
                    partners[rank_of(core, y, z)] = partner_of(exchange_plan(stream, core)[step], core, y, z)
        steps.append(partners)
    return steps


def block_order(stream):
    steps = exchange_partners(stream)
    order = {rank: [rank % SEQ] for rank in range(RANKS)}
    for partners in reversed(steps):
        order = {rank: order[rank] + order[partners[rank]] for rank in range(RANKS)}
    for rank in range(RANKS):
        assert sorted(order[rank]) == list(range(SEQ))
    return np.array([order[rank] for rank in range(RANKS)], np.int32)


PARTNERS = [exchange_partners(stream) for stream in range(2)]
ORDERS = np.stack([block_order(stream) for stream in range(2)])


def dot(a, b, contract):
    return lax.dot_general(a, b, ((contract[:1], contract[1:]), ((), ())), preferred_element_type=F32)


def split3(value):
    high = value.astype(BF16)
    rest = value - high.astype(F32)
    middle = rest.astype(BF16)
    low = (rest - middle.astype(F32)).astype(BF16)
    return high, middle, low


def moves(sources, targets, semaphores, first=0):
    return [
        pltpu.make_async_copy(source, target, semaphores.at[first + at])
        for at, (source, target) in enumerate(zip(sources, targets))
    ]


def start_all(copies):
    for copy in copies:
        copy.start()


def prefix_sums(decay):
    heads, tokens = decay.shape
    rows = lax.broadcasted_iota(jnp.int32, (tokens, tokens), 0)
    columns = lax.broadcasted_iota(jnp.int32, (tokens, tokens), 1)
    lower = jnp.where(rows >= columns, 1.0, 0.0).astype(BF16)
    parts = jnp.concatenate([piece.astype(F32) for piece in split3(decay)], axis=0).astype(BF16)
    down = dot(lower, parts, (1, 1))
    across = dot(parts, lower, (1, 1))
    return (
        down[:, :heads] + down[:, heads : 2 * heads] + down[:, 2 * heads :],
        across[:heads] + across[heads : 2 * heads] + across[2 * heads :],
    )


def states_kernel(
    decay_hbm, query_hbm, key_hbm, value_hbm, grad_hbm, out_ref,
    decay_ref, query_ref, key_ref, value_ref, grad_ref, semaphores,
):
    heads, tokens = decay_ref.shape
    scaling = HEAD ** (-0.5)
    copies = moves(
        (decay_hbm, key_hbm, value_hbm, query_hbm, grad_hbm),
        (decay_ref, key_ref, value_ref, query_ref, grad_ref),
        semaphores,
    )
    start_all(copies)
    copies[0].wait()
    cumulative, _ = prefix_sums(decay_ref[...])
    total = cumulative[tokens - 1 :, :]
    from_start = jnp.exp(cumulative)
    to_end = jnp.exp(total - cumulative)
    per = SEQ // (2 * heads)
    span = HEAD // per
    line = lax.broadcasted_iota(jnp.int32, (MESSAGE - span, HEAD), 0)
    tails = []
    for head in range(heads):
        marks = split3(jnp.broadcast_to(total[:, head : head + 1], (MESSAGE - span, HEAD)))
        tail = jnp.where(
            line == 0, marks[0].astype(F32), jnp.where(line == 1, marks[1].astype(F32), marks[2].astype(F32))
        )
        tails.append(jnp.where(line < 3, tail, 0.0).astype(BF16))

    def emit(direction, head, state):
        state = state.astype(BF16)
        for piece in range(per):
            owner = (direction * heads + head) * per + piece
            out_ref[owner, :span, :] = state[piece * span : (piece + 1) * span, :]
            out_ref[owner, span:, :] = tails[head]

    copies[1].wait()
    copies[2].wait()
    for head in range(heads):
        part = slice(head * HEAD, (head + 1) * HEAD)
        x = key_ref[:, part].astype(F32)
        weighted = (x * jax.nn.sigmoid(x) * to_end[:, head : head + 1]).astype(BF16)
        emit(0, head, dot(weighted, value_ref[:, part], (0, 0)))
    copies[3].wait()
    copies[4].wait()
    for head in range(heads):
        part = slice(head * HEAD, (head + 1) * HEAD)
        x = query_ref[:, part].astype(F32)
        weighted = (x * jax.nn.sigmoid(x) * (scaling * from_start[:, head : head + 1])).astype(BF16)
        emit(1, head, dot(weighted, grad_ref[:, part], (0, 0)))


def scan_kernel(place_ref, in_ref, out_ref):
    count = in_ref.shape[0]
    span = out_ref.shape[1]
    backward = place_ref[0] >= count // 2

    def step(at, carried):
        source = jnp.where(backward, count - 1 - at, at)
        out_ref[source] = carried.astype(BF16)
        message = in_ref[source].astype(F32)
        total = message[span : span + 1] + message[span + 1 : span + 2] + message[span + 2 : span + 3]
        return jnp.exp(total) * carried + message[:span]

    lax.fori_loop(0, count, step, jnp.zeros((span, HEAD), F32), unroll=4)


def local_kernel(
    decay_hbm, query_hbm, key_hbm, value_hbm, grad_hbm,
    gq_hbm, gk_hbm, gv_hbm, sq_hbm, sk_hbm, wo_hbm, wv_hbm, wk_hbm,
    decay_ref, query_ref, key_ref, value_ref, grad_ref,
    q_ref, k_ref, gq_ref, gk_ref, gv_ref, sq_ref, sk_ref, wo_ref, wv_ref, wk_ref, cum_ref, row_ref, semaphores,
):
    heads, tokens = decay_ref.shape
    scaling = HEAD ** (-0.5)
    copies = moves(
        (decay_hbm, query_hbm, key_hbm, value_hbm, grad_hbm),
        (decay_ref, query_ref, key_ref, value_ref, grad_ref),
        semaphores,
    )
    start_all(copies)
    writes = moves(
        (gq_ref, gk_ref, gv_ref, sq_ref, sk_ref, wo_ref, wv_ref, wk_ref),
        (gq_hbm, gk_hbm, gv_hbm, sq_hbm, sk_hbm, wo_hbm, wv_hbm, wk_hbm),
        semaphores,
        len(copies),
    )
    copies[0].wait()
    cum_ref[...], row_ref[...] = prefix_sums(decay_ref[...])
    for copy in copies[1:]:
        copy.wait()
    half = tokens // 2
    rows = lax.broadcasted_iota(jnp.int32, (half, half), 0)
    columns = lax.broadcasted_iota(jnp.int32, (half, half), 1)
    causal = rows >= columns
    for head in range(heads):
        part = slice(head * HEAD, (head + 1) * HEAD)
        line = slice(head, head + 1)
        x = query_ref[:, part].astype(F32)
        sigmoid = jax.nn.sigmoid(x)
        q_ref[:, part] = (x * sigmoid * scaling).astype(BF16)
        sq_ref[:, part] = (sigmoid * (1.0 + x * (1.0 - sigmoid)) * scaling).astype(BF16)
        x = key_ref[:, part].astype(F32)
        sigmoid = jax.nn.sigmoid(x)
        keys = (x * sigmoid).astype(BF16)
        k_ref[:, part] = keys
        sk_ref[:, part] = (sigmoid * (1.0 + x * (1.0 - sigmoid))).astype(BF16)
        cumulative = cum_ref[:, line]
        to_end = jnp.exp(cum_ref[tokens - 1 :, line] - cumulative)
        wo_ref[:, part] = (jnp.exp(cumulative) * grad_ref[:, part].astype(F32)).astype(BF16)
        wv_ref[:, part] = (to_end * value_ref[:, part].astype(F32)).astype(BF16)
        wk_ref[:, part] = (to_end * keys.astype(F32)).astype(BF16)

        def diagonal(block):
            spread = cum_ref[block, line] - row_ref[line, block]
            return jnp.where(causal, jnp.exp(jnp.minimum(spread, 0.0)), 0.0)

        early, late = slice(0, half), slice(half, tokens)
        border = cum_ref[half - 1 : half, line]
        decay_first = diagonal(early)
        decay_last = diagonal(late)
        decay_rows = jnp.exp(jnp.minimum(cum_ref[late, line] - border, 0.0))
        decay_columns = jnp.exp(jnp.minimum(border - row_ref[line, early], 0.0))

        def scores(left, right):
            first = (dot(left[early, part], right[early, part], (1, 1)) * decay_first).astype(BF16)
            across = (dot(left[late, part], right[early, part], (1, 1)) * decay_rows * decay_columns).astype(BF16)
            last = (dot(left[late, part], right[late, part], (1, 1)) * decay_last).astype(BF16)
            return first, across, last

        first, across, last = scores(grad_ref, value_ref)
        gq_ref[early, part] = dot(first, k_ref[early, part], (1, 0)).astype(BF16)
        gq_ref[late, part] = (dot(across, k_ref[early, part], (1, 0)) + dot(last, k_ref[late, part], (1, 0))).astype(BF16)
        gk_ref[early, part] = (dot(first, q_ref[early, part], (0, 0)) + dot(across, q_ref[late, part], (0, 0))).astype(BF16)
        gk_ref[late, part] = dot(last, q_ref[late, part], (0, 0)).astype(BF16)
        first, across, last = scores(q_ref, k_ref)
        gv_ref[early, part] = dot(first, grad_ref[early, part], (0, 0)) + dot(across, grad_ref[late, part], (0, 0))
        gv_ref[late, part] = dot(last, grad_ref[late, part], (0, 0))
    start_all(writes)
    for copy in writes:
        copy.wait()


def heads_kernel(
    states_hbm, wo_hbm, gq_hbm, sq_hbm, wv_hbm, gk_hbm, sk_hbm,
    slopes_q_ref, slopes_k_ref,
    states_ref, wo_ref, gq_ref, sq_ref, wv_ref, gk_ref, sk_ref, semaphores,
):
    heads = wo_ref.shape[1] // HEAD
    copies = moves(
        (wo_hbm, states_hbm, gq_hbm, sq_hbm, wv_hbm, gk_hbm, sk_hbm),
        (wo_ref, states_ref, gq_ref, sq_ref, wv_ref, gk_ref, sk_ref),
        semaphores,
    )
    start_all(copies)
    for stream, (weighted, local, slope, slopes) in enumerate(
        ((wo_ref, gq_ref, sq_ref, slopes_q_ref), (wv_ref, gk_ref, sk_ref, slopes_k_ref))
    ):
        for copy in copies[4 * stream : 4 * stream + 4 - stream]:
            copy.wait()
        for head in range(heads):
            part = slice(head * HEAD, (head + 1) * HEAD)
            state = slice((stream * heads + head) * HEAD, (stream * heads + head + 1) * HEAD)
            gradient = local[:, part].astype(F32) + dot(weighted[:, part], states_ref[state, :], (1, 1))
            slopes[:, part] = (gradient * slope[:, part].astype(F32)).astype(BF16)


def pair_kernel(own_ref, rows_ref, slopes_ref, *refs, first):
    out_ref = refs[-1]
    part = slice(first, first + out_ref.shape[0])
    out_ref[...] = (own_ref[part] + dot(rows_ref[...], slopes_ref[...], (1, 0))).astype(out_ref.dtype)


def values_kernel(local_ref, weighted_ref, states_ref, out_ref):
    heads = out_ref.shape[1] // HEAD
    for head in range(heads):
        part = slice(head * HEAD, (head + 1) * HEAD)
        later = slice((heads + head) * HEAD, (heads + head + 1) * HEAD)
        out_ref[:, part] = (local_ref[:, part] + dot(weighted_ref[:, part], states_ref[later, :], (1, 0))).astype(BF16)


def arrange_kernel(
    place_ref, table_ref, input_hbm,
    late0_hbm, late1_hbm, early0_hbm, early1_hbm, kept0_hbm, kept1_hbm,
    input_ref, turned_ref, late0_ref, late1_ref, early0_ref, early1_ref, kept0_ref, kept1_ref, semaphores,
):
    tokens, width = input_ref.shape
    block = width // SEQ
    chunk = 384
    reads = moves(
        [input_hbm.at[:, at : at + chunk] for at in range(0, width, chunk)],
        [input_ref.at[:, at : at + chunk] for at in range(0, width, chunk)],
        semaphores,
    )
    start_all(reads)
    outs = (late0_ref, late1_ref, early0_ref, early1_ref, kept0_ref, kept1_ref)
    targets = (late0_hbm, late1_hbm, early0_hbm, early1_hbm, kept0_hbm, kept1_hbm)
    writes = moves(outs, targets, semaphores, len(reads))
    for at, copy in enumerate(reads):
        copy.wait()
        turned_ref[at * chunk : (at + 1) * chunk, :] = input_ref[:, at * chunk : (at + 1) * chunk].T
    firsts = (3 * SEQ // 4, 3 * SEQ // 4, SEQ // 2, SEQ // 2, 0, 0)
    for out, write, stream, first in zip(outs, writes, (0, 1) * 3, firsts):
        for at in range(out.shape[0] // block):
            entry = (stream * RANKS + place_ref[0]) * SEQ + first + at
            start = pl.multiple_of(table_ref[entry] * block, block)
            out[at * block : (at + 1) * block, :] = turned_ref[pl.ds(start, block), :]
        write.start()
    for copy in writes:
        copy.wait()


def own_kernel(
    rows0_hbm, rows1_hbm, slopes0_ref, slopes1_ref, out0_ref, out1_ref, rows0_ref, rows1_ref, semaphores
):
    copies = moves((rows0_hbm, rows1_hbm), (rows0_ref, rows1_ref), semaphores)
    start_all(copies)
    for copy, rows, slopes, out in zip(
        copies, (rows0_ref, rows1_ref), (slopes0_ref, slopes1_ref), (out0_ref, out1_ref)
    ):
        copy.wait()
        out[...] = dot(rows[...], slopes[...], (1, 0))


def add_kernel(received_ref, kept_ref, keep_ref, send_ref):
    half = keep_ref.shape[0]
    keep_ref[...] = kept_ref[:half] + received_ref[:half].astype(F32)
    send_ref[...] = (kept_ref[half:] + received_ref[half:].astype(F32)).astype(BF16)


def last_one_kernel(received_ref, kept_ref, mark_ref, out_ref):
    out_ref[...] = kept_ref[...] + received_ref[...].astype(F32)


def shaped(shape, dtype):
    return jax.ShapeDtypeStruct(shape, dtype)


def cost(flops, moved):
    return pl.CostEstimate(flops=flops, bytes_accessed=moved, transcendentals=0)


IN_HBM = pl.BlockSpec(memory_space=pltpu.HBM)
IN_VMEM = pl.BlockSpec(memory_space=pltpu.VMEM)


def per_device(layer_input, query_preact, key_preact, value_rows, output_grad, log_decay):
    tokens, heads = log_decay.shape
    columns = query_preact.shape[1]
    width = layer_input.shape[1]
    core, y, z = (lax.axis_index(axis) for axis in AXES)
    place = y * N_Z + z
    half = width // 2
    small, large = shaped((tokens, columns), BF16), shaped((tokens, columns), F32)
    partial = shaped((half, columns), BF16)
    turned = shaped((half, tokens), BF16)
    decay = shaped((heads, tokens), F32)
    states_shape = shaped((2 * heads * HEAD, HEAD), BF16)
    arguments = (log_decay.T, query_preact, key_preact, value_rows, output_grad)

    def scratch(*shapes):
        return [pltpu.VMEM(one.shape, one.dtype) for one in shapes]

    def semaphores(count):
        return [pltpu.SemaphoreType.DMA((count,))]

    states = pl.pallas_call(
        states_kernel,
        in_specs=[IN_HBM] * 5,
        out_shape=shaped((SEQ, MESSAGE, HEAD), BF16),
        scratch_shapes=scratch(decay, small, small, small, small) + semaphores(5),
        compiler_params=WIDE,
        cost_estimate=cost(10**9, 4 * 10**6),
    )(*arguments)
    states = lax.all_to_all(states, ("y", "z"), 0, 0, tiled=True)
    local_shapes = (small, small, large, small, small, small, small, small)
    local_q, local_k, local_v, slope_q, slope_k, weighted_o, weighted_v, weighted_k = pl.pallas_call(
        local_kernel,
        in_specs=[IN_HBM] * 5,
        out_specs=(IN_HBM,) * 8,
        out_shape=local_shapes,
        scratch_shapes=scratch(decay, *(small,) * 6, *local_shapes, shaped((tokens, heads), F32), decay)
        + semaphores(13),
        compiler_params=WIDE,
        cost_estimate=cost(6 * 10**10, 10**7),
    )(*arguments)
    rank = (core * SEQ + place)[None].astype(jnp.int32)
    table = jnp.asarray(ORDERS.reshape(-1))
    chunks = width // 384

    quarter = shaped((half // 2, tokens), BF16)
    arranged = (quarter,) * 4 + (turned,) * 2
    late0, late1, early0, early1, kept0, kept1 = pl.pallas_call(
        arrange_kernel,
        in_specs=[pl.BlockSpec(memory_space=pltpu.SMEM)] * 2 + [IN_HBM],
        out_specs=(IN_HBM,) * 6,
        out_shape=arranged,
        scratch_shapes=scratch(shaped((tokens, width), BF16), shaped((width, tokens), BF16), *arranged)
        + semaphores(chunks + 6),
        compiler_params=WIDE,
        cost_estimate=cost(10**9, 10**7),
    )(rank, table, layer_input)
    states, kept0 = lax.optimization_barrier((states, kept0))
    span = 2 * heads * HEAD // SEQ
    incoming = pl.pallas_call(
        scan_kernel,
        in_specs=[pl.BlockSpec(memory_space=pltpu.SMEM), IN_VMEM],
        out_shape=shaped((SEQ, span, HEAD), BF16),
        compiler_params=VMEM,
    )(place[None].astype(jnp.int32), states)
    incoming, early0, early1 = lax.optimization_barrier((incoming, early0, early1))
    incoming = lax.all_to_all(incoming, ("y", "z"), 0, 0, tiled=True).reshape(2 * heads * HEAD, HEAD)
    flops = 2 * half * columns * tokens

    def exchange(stream, step, array):
        return lax.ppermute(array, AXES, sorted(PARTNERS[stream][step].items()))

    late0, late1 = exchange(0, 0, late0), exchange(1, 0, late1)
    early0, early1 = exchange(0, 0, early0), exchange(1, 0, early1)
    early0, early1, kept0 = lax.optimization_barrier((early0, early1, kept0))
    slopes_q, slopes_k = pl.pallas_call(
        heads_kernel,
        in_specs=[pl.BlockSpec(memory_space=pl.ANY)] + [IN_HBM] * 6,
        out_shape=(small, small),
        scratch_shapes=scratch(states_shape, *(small,) * 6) + semaphores(7),
        compiler_params=WIDE,
        cost_estimate=cost(10**9, 4 * 10**6),
    )(incoming, weighted_o, local_q, slope_q, weighted_v, local_k, slope_k)
    partner_q, partner_k = exchange(0, 0, slopes_q), exchange(1, 0, slopes_k)
    own0, own1 = pl.pallas_call(
        own_kernel,
        in_specs=[IN_HBM, IN_HBM, IN_VMEM, IN_VMEM],
        out_shape=(shaped((half, columns), F32),) * 2,
        scratch_shapes=scratch(turned, turned) + semaphores(2),
        compiler_params=VMEM,
        cost_estimate=cost(2 * flops, 10**7),
    )(kept0, kept1, slopes_q, slopes_k)
    rows = half // 2

    def paired(first, dtype, *operands):
        return pl.pallas_call(
            functools.partial(pair_kernel, first=first),
            in_specs=[IN_VMEM] * 3 + [IN_HBM] * (len(operands) - 3),
            out_shape=shaped((rows, columns), dtype),
            compiler_params=VMEM,
            cost_estimate=cost(flops // 2, 3 * 10**6),
        )(*operands)

    send0 = paired(rows, BF16, own0, late0, partner_q)
    send1 = paired(rows, BF16, own1, late1, partner_k)
    after = send1[:16, :128]
    keep0 = paired(0, F32, own0, early0, partner_q, after)
    keep1 = paired(0, F32, own1, early1, partner_k, after)
    keeps, sends = [keep0, keep1], [send0, send1]
    for step in range(1, STEPS - 1):
        received = [exchange(stream, step, sends[stream]) for stream in range(2)]
        rows //= 2
        if step < STEPS - 2:
            pairs = [
                pl.pallas_call(
                    add_kernel,
                    out_shape=(shaped((rows, columns), F32), shaped((rows, columns), BF16)),
                    compiler_params=VMEM,
                )(received[stream], keeps[stream])
                for stream in range(2)
            ]
            keeps, sends = [one[0] for one in pairs], [one[1] for one in pairs]
        else:
            pairs = [
                pl.pallas_call(
                    add_kernel,
                    out_shape=(shaped((rows, columns), F32), shaped((rows, columns), BF16)),
                    compiler_params=VMEM,
                )(received[stream], keeps[stream])
                for stream in range(2)
            ]
            keeps, sends = [one[0] for one in pairs], [one[1] for one in pairs]
    other_core = [(rank, (rank + SEQ) % RANKS) for rank in range(RANKS)]
    mark = lax.ppermute(sends[1][:16, :128], AXES, other_core)
    gated, mark = lax.optimization_barrier((sends[0], mark))
    sends = (gated, sends[1], mark)
    kweight_grad = pl.pallas_call(
        last_one_kernel,
        in_specs=[IN_VMEM, IN_VMEM, pl.BlockSpec(memory_space=pl.ANY)],
        out_shape=shaped((rows, columns), F32),
        compiler_params=VMEM,
    )(exchange(1, STEPS - 1, sends[1]), keeps[1], sends[2])
    qweight_grad = keeps[0] + exchange(0, STEPS - 1, sends[0]).astype(F32)
    value_grad = pl.pallas_call(
        values_kernel,
        out_shape=small,
        compiler_params=VMEM,
        cost_estimate=cost(10**9, 5 * 10**6),
    )(local_v, weighted_k, incoming)
    return qweight_grad, kweight_grad, value_grad


def solution(mesh):
    chips = mesh.devices.shape[0] // CORES
    split = Mesh(mesh.devices.reshape(chips, CORES, N_Y, N_Z), ("x",) + AXES)
    seq, cores = ("y", "z"), ("x", "core")
    both = P(seq, cores)
    return jax.shard_map(
        per_device,
        mesh=split,
        in_specs=(P(seq, None), both, both, both, both, both),
        out_specs=(both, both, both),
        check_vma=False,
    )
```

```python
import functools

import jax
import jax.numpy as jnp
import numpy as np
from jax import lax
from jax.experimental import pallas as pl
from jax.experimental.pallas import tpu as pltpu
from jax.sharding import Mesh, PartitionSpec as P

HEAD = 128
N_Y = 4
N_Z = 8
SEQ = N_Y * N_Z
CORES = 2
RANKS = CORES * SEQ
STEPS = 5
AXES = ("core", "y", "z")
MESSAGE = 40
BF16 = jnp.bfloat16
F32 = jnp.float32
VMEM = pltpu.CompilerParams(vmem_limit_bytes=20 * 2**20)
WIDE = pltpu.CompilerParams(vmem_limit_bytes=56 * 2**20)


def exchange_plan(stream, core):
    way = 1 - 2 * core
    if stream == 0:
        return [("z", way), ("y", way), ("y", -way), ("z", -way), ("z", 3 * way)]
    return [("y", way), ("z", way), ("z", -way), ("y", -way), ("z", 3 * way)]


def rank_of(core, y, z):
    return (core * N_Y + y) * N_Z + z


def partner_of(kind, core, y, z):
    axis, shift = kind
    if axis == "z":
        return rank_of(core, y, (z + shift * (1 - 2 * (z % 2))) % N_Z)
    return rank_of(core, (y + shift * (1 - 2 * (y % 2))) % N_Y, z)


def exchange_partners(stream):
    steps = []
    for step in range(STEPS):
        partners = {}
        for core in range(CORES):
            for y in range(N_Y):
                for z in range(N_Z):
                    partners[rank_of(core, y, z)] = partner_of(exchange_plan(stream, core)[step], core, y, z)
        steps.append(partners)
    return steps


def block_order(stream):
    steps = exchange_partners(stream)
    order = {rank: [rank % SEQ] for rank in range(RANKS)}
    for partners in reversed(steps):
        order = {rank: order[rank] + order[partners[rank]] for rank in range(RANKS)}
    for rank in range(RANKS):
        assert sorted(order[rank]) == list(range(SEQ))
    return np.array([order[rank] for rank in range(RANKS)], np.int32)


PARTNERS = [exchange_partners(stream) for stream in range(2)]
ORDERS = np.stack([block_order(stream) for stream in range(2)])


def dot(a, b, contract):
    return lax.dot_general(a, b, ((contract[:1], contract[1:]), ((), ())), preferred_element_type=F32)


def split3(value):
    high = value.astype(BF16)
    rest = value - high.astype(F32)
    middle = rest.astype(BF16)
    low = (rest - middle.astype(F32)).astype(BF16)
    return high, middle, low


def moves(sources, targets, semaphores, first=0):
    return [
        pltpu.make_async_copy(source, target, semaphores.at[first + at])
        for at, (source, target) in enumerate(zip(sources, targets))
    ]


def start_all(copies):
    for copy in copies:
        copy.start()


def prefix_sums(decay):
    heads, tokens = decay.shape
    rows = lax.broadcasted_iota(jnp.int32, (tokens, tokens), 0)
    columns = lax.broadcasted_iota(jnp.int32, (tokens, tokens), 1)
    lower = jnp.where(rows >= columns, 1.0, 0.0).astype(BF16)
    parts = jnp.concatenate([piece.astype(F32) for piece in split3(decay)], axis=0).astype(BF16)
    down = dot(lower, parts, (1, 1))
    across = dot(parts, lower, (1, 1))
    return (
        down[:, :heads] + down[:, heads : 2 * heads] + down[:, 2 * heads :],
        across[:heads] + across[heads : 2 * heads] + across[2 * heads :],
    )


def states_kernel(
    decay_hbm, query_hbm, key_hbm, value_hbm, grad_hbm, out_ref,
    decay_ref, query_ref, key_ref, value_ref, grad_ref, semaphores,
):
    heads, tokens = decay_ref.shape
    scaling = HEAD ** (-0.5)
    copies = moves(
        (decay_hbm, key_hbm, value_hbm, query_hbm, grad_hbm),
        (decay_ref, key_ref, value_ref, query_ref, grad_ref),
        semaphores,
    )
    start_all(copies)
    copies[0].wait()
    cumulative, _ = prefix_sums(decay_ref[...])
    total = cumulative[tokens - 1 :, :]
    from_start = jnp.exp(cumulative)
    to_end = jnp.exp(total - cumulative)
    per = SEQ // (2 * heads)
    span = HEAD // per
    line = lax.broadcasted_iota(jnp.int32, (MESSAGE - span, HEAD), 0)
    tails = []
    for head in range(heads):
        marks = split3(jnp.broadcast_to(total[:, head : head + 1], (MESSAGE - span, HEAD)))
        tail = jnp.where(
            line == 0, marks[0].astype(F32), jnp.where(line == 1, marks[1].astype(F32), marks[2].astype(F32))
        )
        tails.append(jnp.where(line < 3, tail, 0.0).astype(BF16))

    def emit(direction, head, state):
        state = state.astype(BF16)
        for piece in range(per):
            owner = (direction * heads + head) * per + piece
            out_ref[owner, :span, :] = state[piece * span : (piece + 1) * span, :]
            out_ref[owner, span:, :] = tails[head]

    copies[1].wait()
    copies[2].wait()
    for head in range(heads):
        part = slice(head * HEAD, (head + 1) * HEAD)
        x = key_ref[:, part].astype(F32)
        weighted = (x * jax.nn.sigmoid(x) * to_end[:, head : head + 1]).astype(BF16)
        emit(0, head, dot(weighted, value_ref[:, part], (0, 0)))
    copies[3].wait()
    copies[4].wait()
    for head in range(heads):
        part = slice(head * HEAD, (head + 1) * HEAD)
        x = query_ref[:, part].astype(F32)
        weighted = (x * jax.nn.sigmoid(x) * (scaling * from_start[:, head : head + 1])).astype(BF16)
        emit(1, head, dot(weighted, grad_ref[:, part], (0, 0)))


def scan_kernel(place_ref, in_ref, out_ref):
    count = in_ref.shape[0]
    span = out_ref.shape[1]
    backward = place_ref[0] >= count // 2

    def step(at, carried):
        source = jnp.where(backward, count - 1 - at, at)
        out_ref[source] = carried.astype(BF16)
        message = in_ref[source].astype(F32)
        total = message[span : span + 1] + message[span + 1 : span + 2] + message[span + 2 : span + 3]
        return jnp.exp(total) * carried + message[:span]

    lax.fori_loop(0, count, step, jnp.zeros((span, HEAD), F32), unroll=4)


def local_kernel(
    decay_hbm, query_hbm, key_hbm, value_hbm, grad_hbm,
    gq_hbm, gk_hbm, gv_hbm, sq_hbm, sk_hbm, wo_hbm, wv_hbm, wk_hbm,
    decay_ref, query_ref, key_ref, value_ref, grad_ref,
    q_ref, k_ref, gq_ref, gk_ref, gv_ref, sq_ref, sk_ref, wo_ref, wv_ref, wk_ref, cum_ref, row_ref, semaphores,
):
    heads, tokens = decay_ref.shape
    scaling = HEAD ** (-0.5)
    copies = moves(
        (decay_hbm, query_hbm, key_hbm, value_hbm, grad_hbm),
        (decay_ref, query_ref, key_ref, value_ref, grad_ref),
        semaphores,
    )
    start_all(copies)
    writes = moves(
        (gq_ref, gk_ref, gv_ref, sq_ref, sk_ref, wo_ref, wv_ref, wk_ref),
        (gq_hbm, gk_hbm, gv_hbm, sq_hbm, sk_hbm, wo_hbm, wv_hbm, wk_hbm),
        semaphores,
        len(copies),
    )
    copies[0].wait()
    cum_ref[...], row_ref[...] = prefix_sums(decay_ref[...])
    for copy in copies[1:]:
        copy.wait()
    half = tokens // 2
    rows = lax.broadcasted_iota(jnp.int32, (half, half), 0)
    columns = lax.broadcasted_iota(jnp.int32, (half, half), 1)
    causal = rows >= columns
    for head in range(heads):
        part = slice(head * HEAD, (head + 1) * HEAD)
        line = slice(head, head + 1)
        x = query_ref[:, part].astype(F32)
        sigmoid = jax.nn.sigmoid(x)
        q_ref[:, part] = (x * sigmoid * scaling).astype(BF16)
        sq_ref[:, part] = (sigmoid * (1.0 + x * (1.0 - sigmoid)) * scaling).astype(BF16)
        x = key_ref[:, part].astype(F32)
        sigmoid = jax.nn.sigmoid(x)
        keys = (x * sigmoid).astype(BF16)
        k_ref[:, part] = keys
        sk_ref[:, part] = (sigmoid * (1.0 + x * (1.0 - sigmoid))).astype(BF16)
        cumulative = cum_ref[:, line]
        to_end = jnp.exp(cum_ref[tokens - 1 :, line] - cumulative)
        wo_ref[:, part] = (jnp.exp(cumulative) * grad_ref[:, part].astype(F32)).astype(BF16)
        wv_ref[:, part] = (to_end * value_ref[:, part].astype(F32)).astype(BF16)
        wk_ref[:, part] = (to_end * keys.astype(F32)).astype(BF16)

        def diagonal(block):
            spread = cum_ref[block, line] - row_ref[line, block]
            return jnp.where(causal, jnp.exp(jnp.minimum(spread, 0.0)), 0.0)

        early, late = slice(0, half), slice(half, tokens)
        border = cum_ref[half - 1 : half, line]
        decay_first = diagonal(early)
        decay_last = diagonal(late)
        decay_rows = jnp.exp(jnp.minimum(cum_ref[late, line] - border, 0.0))
        decay_columns = jnp.exp(jnp.minimum(border - row_ref[line, early], 0.0))

        def scores(left, right):
            first = (dot(left[early, part], right[early, part], (1, 1)) * decay_first).astype(BF16)
            across = (dot(left[late, part], right[early, part], (1, 1)) * decay_rows * decay_columns).astype(BF16)
            last = (dot(left[late, part], right[late, part], (1, 1)) * decay_last).astype(BF16)
            return first, across, last

        first, across, last = scores(grad_ref, value_ref)
        gq_ref[early, part] = dot(first, k_ref[early, part], (1, 0)).astype(BF16)
        gq_ref[late, part] = (dot(across, k_ref[early, part], (1, 0)) + dot(last, k_ref[late, part], (1, 0))).astype(BF16)
        gk_ref[early, part] = (dot(first, q_ref[early, part], (0, 0)) + dot(across, q_ref[late, part], (0, 0))).astype(BF16)
        gk_ref[late, part] = dot(last, q_ref[late, part], (0, 0)).astype(BF16)
        first, across, last = scores(q_ref, k_ref)
        gv_ref[early, part] = dot(first, grad_ref[early, part], (0, 0)) + dot(across, grad_ref[late, part], (0, 0))
        gv_ref[late, part] = dot(last, grad_ref[late, part], (0, 0))
    start_all(writes)
    for copy in writes:
        copy.wait()


def heads_kernel(
    states_hbm, wo_hbm, gq_hbm, sq_hbm, wv_hbm, gk_hbm, sk_hbm,
    slopes_q_ref, slopes_k_ref,
    states_ref, wo_ref, gq_ref, sq_ref, wv_ref, gk_ref, sk_ref, semaphores,
):
    heads = wo_ref.shape[1] // HEAD
    copies = moves(
        (wo_hbm, states_hbm, gq_hbm, sq_hbm, wv_hbm, gk_hbm, sk_hbm),
        (wo_ref, states_ref, gq_ref, sq_ref, wv_ref, gk_ref, sk_ref),
        semaphores,
    )
    start_all(copies)
    for stream, (weighted, local, slope, slopes) in enumerate(
        ((wo_ref, gq_ref, sq_ref, slopes_q_ref), (wv_ref, gk_ref, sk_ref, slopes_k_ref))
    ):
        for copy in copies[4 * stream : 4 * stream + 4 - stream]:
            copy.wait()
        for head in range(heads):
            part = slice(head * HEAD, (head + 1) * HEAD)
            state = slice((stream * heads + head) * HEAD, (stream * heads + head + 1) * HEAD)
            gradient = local[:, part].astype(F32) + dot(weighted[:, part], states_ref[state, :], (1, 1))
            slopes[:, part] = (gradient * slope[:, part].astype(F32)).astype(BF16)


def pair_kernel(own_ref, rows_ref, slopes_ref, *refs, first):
    out_ref = refs[-1]
    part = slice(first, first + out_ref.shape[0])
    out_ref[...] = (own_ref[part] + dot(rows_ref[...], slopes_ref[...], (1, 0))).astype(out_ref.dtype)


def values_kernel(local_ref, weighted_ref, states_ref, out_ref):
    heads = out_ref.shape[1] // HEAD
    for head in range(heads):
        part = slice(head * HEAD, (head + 1) * HEAD)
        later = slice((heads + head) * HEAD, (heads + head + 1) * HEAD)
        out_ref[:, part] = (local_ref[:, part] + dot(weighted_ref[:, part], states_ref[later, :], (1, 0))).astype(BF16)


def arrange_kernel(
    place_ref, table_ref, input_hbm,
    late0_hbm, late1_hbm, early0_hbm, early1_hbm, kept0_hbm, kept1_hbm,
    input_ref, turned_ref, late0_ref, late1_ref, early0_ref, early1_ref, kept0_ref, kept1_ref, semaphores,
):
    tokens, width = input_ref.shape
    block = width // SEQ
    chunk = 384
    reads = moves(
        [input_hbm.at[:, at : at + chunk] for at in range(0, width, chunk)],
        [input_ref.at[:, at : at + chunk] for at in range(0, width, chunk)],
        semaphores,
    )
    start_all(reads)
    outs = (late0_ref, late1_ref, early0_ref, early1_ref, kept0_ref, kept1_ref)
    targets = (late0_hbm, late1_hbm, early0_hbm, early1_hbm, kept0_hbm, kept1_hbm)
    writes = moves(outs, targets, semaphores, len(reads))
    for at, copy in enumerate(reads):
        copy.wait()
        turned_ref[at * chunk : (at + 1) * chunk, :] = input_ref[:, at * chunk : (at + 1) * chunk].T
    firsts = (3 * SEQ // 4, 3 * SEQ // 4, SEQ // 2, SEQ // 2, 0, 0)
    for out, write, stream, first in zip(outs, writes, (0, 1) * 3, firsts):
        for at in range(out.shape[0] // block):
            entry = (stream * RANKS + place_ref[0]) * SEQ + first + at
            start = pl.multiple_of(table_ref[entry] * block, block)
            out[at * block : (at + 1) * block, :] = turned_ref[pl.ds(start, block), :]
        write.start()
    for copy in writes:
        copy.wait()


def own_kernel(
    rows0_hbm, rows1_hbm, slopes0_ref, slopes1_ref, out0_ref, out1_ref, rows0_ref, rows1_ref, semaphores
):
    copies = moves((rows0_hbm, rows1_hbm), (rows0_ref, rows1_ref), semaphores)
    start_all(copies)
    for copy, rows, slopes, out in zip(
        copies, (rows0_ref, rows1_ref), (slopes0_ref, slopes1_ref), (out0_ref, out1_ref)
    ):
        copy.wait()
        out[...] = dot(rows[...], slopes[...], (1, 0))


def add_kernel(received_ref, kept_ref, keep_ref, send_ref):
    half = keep_ref.shape[0]
    keep_ref[...] = kept_ref[:half] + received_ref[:half].astype(F32)
    send_ref[...] = (kept_ref[half:] + received_ref[half:].astype(F32)).astype(BF16)


def last_one_kernel(received_ref, kept_ref, mark_ref, out_ref):
    out_ref[...] = kept_ref[...] + received_ref[...].astype(F32)


def shaped(shape, dtype):
    return jax.ShapeDtypeStruct(shape, dtype)


def cost(flops, moved):
    return pl.CostEstimate(flops=flops, bytes_accessed=moved, transcendentals=0)


IN_HBM = pl.BlockSpec(memory_space=pltpu.HBM)
IN_VMEM = pl.BlockSpec(memory_space=pltpu.VMEM)


def per_device(layer_input, query_preact, key_preact, value_rows, output_grad, log_decay):
    tokens, heads = log_decay.shape
    columns = query_preact.shape[1]
    width = layer_input.shape[1]
    core, y, z = (lax.axis_index(axis) for axis in AXES)
    place = y * N_Z + z
    half = width // 2
    small, large = shaped((tokens, columns), BF16), shaped((tokens, columns), F32)
    partial = shaped((half, columns), BF16)
    turned = shaped((half, tokens), BF16)
    decay = shaped((heads, tokens), F32)
    states_shape = shaped((2 * heads * HEAD, HEAD), BF16)
    arguments = (log_decay.T, query_preact, key_preact, value_rows, output_grad)

    def scratch(*shapes):
        return [pltpu.VMEM(one.shape, one.dtype) for one in shapes]

    def semaphores(count):
        return [pltpu.SemaphoreType.DMA((count,))]

    states = pl.pallas_call(
        states_kernel,
        in_specs=[IN_HBM] * 5,
        out_shape=shaped((SEQ, MESSAGE, HEAD), BF16),
        scratch_shapes=scratch(decay, small, small, small, small) + semaphores(5),
        compiler_params=WIDE,
        cost_estimate=cost(10**9, 4 * 10**6),
    )(*arguments)
    states = lax.all_to_all(states, ("y", "z"), 0, 0, tiled=True)
    local_shapes = (small, small, large, small, small, small, small, small)
    local_q, local_k, local_v, slope_q, slope_k, weighted_o, weighted_v, weighted_k = pl.pallas_call(
        local_kernel,
        in_specs=[IN_HBM] * 5,
        out_specs=(IN_HBM,) * 8,
        out_shape=local_shapes,
        scratch_shapes=scratch(decay, *(small,) * 6, *local_shapes, shaped((tokens, heads), F32), decay)
        + semaphores(13),
        compiler_params=WIDE,
        cost_estimate=cost(6 * 10**10, 10**7),
    )(*arguments)
    rank = (core * SEQ + place)[None].astype(jnp.int32)
    table = jnp.asarray(ORDERS.reshape(-1))
    chunks = width // 384

    quarter = shaped((half // 2, tokens), BF16)
    arranged = (quarter,) * 4 + (turned,) * 2
    late0, late1, early0, early1, kept0, kept1 = pl.pallas_call(
        arrange_kernel,
        in_specs=[pl.BlockSpec(memory_space=pltpu.SMEM)] * 2 + [IN_HBM],
        out_specs=(IN_HBM,) * 6,
        out_shape=arranged,
        scratch_shapes=scratch(shaped((tokens, width), BF16), shaped((width, tokens), BF16), *arranged)
        + semaphores(chunks + 6),
        compiler_params=WIDE,
        cost_estimate=cost(10**9, 10**7),
    )(rank, table, layer_input)
    states, kept0 = lax.optimization_barrier((states, kept0))
    span = 2 * heads * HEAD // SEQ
    incoming = pl.pallas_call(
        scan_kernel,
        in_specs=[pl.BlockSpec(memory_space=pltpu.SMEM), IN_VMEM],
        out_shape=shaped((SEQ, span, HEAD), BF16),
        compiler_params=VMEM,
    )(place[None].astype(jnp.int32), states)
    incoming, early0, early1 = lax.optimization_barrier((incoming, early0, early1))
    incoming = lax.all_to_all(incoming, ("y", "z"), 0, 0, tiled=True).reshape(2 * heads * HEAD, HEAD)
    flops = 2 * half * columns * tokens

    def exchange(stream, step, array):
        return lax.ppermute(array, AXES, sorted(PARTNERS[stream][step].items()))

    late0, late1 = exchange(0, 0, late0), exchange(1, 0, late1)
    early0, early1 = exchange(0, 0, early0), exchange(1, 0, early1)
    early0, early1, kept0 = lax.optimization_barrier((early0, early1, kept0))
    slopes_q, slopes_k = pl.pallas_call(
        heads_kernel,
        in_specs=[pl.BlockSpec(memory_space=pl.ANY)] + [IN_HBM] * 6,
        out_shape=(small, small),
        scratch_shapes=scratch(states_shape, *(small,) * 6) + semaphores(7),
        compiler_params=WIDE,
        cost_estimate=cost(10**9, 4 * 10**6),
    )(incoming, weighted_o, local_q, slope_q, weighted_v, local_k, slope_k)
    partner_q, partner_k = exchange(0, 0, slopes_q), exchange(1, 0, slopes_k)
    own0, own1 = pl.pallas_call(
        own_kernel,
        in_specs=[IN_HBM, IN_HBM, IN_VMEM, IN_VMEM],
        out_shape=(shaped((half, columns), F32),) * 2,
        scratch_shapes=scratch(turned, turned) + semaphores(2),
        compiler_params=VMEM,
        cost_estimate=cost(2 * flops, 10**7),
    )(kept0, kept1, slopes_q, slopes_k)
    rows = half // 2

    def paired(first, dtype, *operands):
        return pl.pallas_call(
            functools.partial(pair_kernel, first=first),
            in_specs=[IN_VMEM] * 3 + [IN_HBM] * (len(operands) - 3),
            out_shape=shaped((rows, columns), dtype),
            compiler_params=VMEM,
            cost_estimate=cost(flops // 2, 3 * 10**6),
        )(*operands)

    send0 = paired(rows, BF16, own0, late0, partner_q)
    send1 = paired(rows, BF16, own1, late1, partner_k)
    after = send1[:16, :128]
    keep0 = paired(0, F32, own0, early0, partner_q, after)
    keep1 = paired(0, F32, own1, early1, partner_k, after)
    keeps, sends = [keep0, keep1], [send0, send1]
    for step in range(1, STEPS - 1):
        received = [exchange(stream, step, sends[stream]) for stream in range(2)]
        rows //= 2
        if step < STEPS - 2:
            pairs = [
                pl.pallas_call(
                    add_kernel,
                    out_shape=(shaped((rows, columns), F32), shaped((rows, columns), BF16)),
                    compiler_params=VMEM,
                )(received[stream], keeps[stream])
                for stream in range(2)
            ]
            keeps, sends = [one[0] for one in pairs], [one[1] for one in pairs]
        else:
            pairs = [
                pl.pallas_call(
                    add_kernel,
                    out_shape=(shaped((rows, columns), F32), shaped((rows, columns), BF16)),
                    compiler_params=VMEM,
                )(received[stream], keeps[stream])
                for stream in range(2)
            ]
            keeps, sends = [one[0] for one in pairs], [one[1] for one in pairs]
    other_core = [(rank, (rank + SEQ) % RANKS) for rank in range(RANKS)]
    mark = lax.ppermute(sends[1][:16, :128], AXES, other_core)
    gated, mark = lax.optimization_barrier((sends[0], mark))
    sends = (gated, sends[1], mark)
    kweight_grad = pl.pallas_call(
        last_one_kernel,
        in_specs=[IN_VMEM, IN_VMEM, pl.BlockSpec(memory_space=pl.ANY)],
        out_shape=shaped((rows, columns), F32),
        compiler_params=VMEM,
    )(exchange(1, STEPS - 1, sends[1]), keeps[1], sends[2])
    qweight_grad = keeps[0] + exchange(0, STEPS - 1, sends[0]).astype(F32)
    value_grad = pl.pallas_call(
        values_kernel,
        out_shape=small,
        compiler_params=VMEM,
        cost_estimate=cost(10**9, 5 * 10**6),
    )(local_v, weighted_k, incoming)
    return qweight_grad, kweight_grad, value_grad


def solution(mesh):
    chips = mesh.devices.shape[0] // CORES
    split = Mesh(mesh.devices.reshape(chips, CORES, N_Y, N_Z), ("x",) + AXES)
    seq, cores = ("y", "z"), ("x", "core")
    both = P(seq, cores)
    return jax.shard_map(
        per_device,
        mesh=split,
        in_specs=(P(seq, None), both, both, both, both, both),
        out_specs=(both, both, both),
        check_vma=False,
    )
```
